256 devices in a mesh: gz: 16 (over z, core), row: 4 (over x), col: 4 (over y).
Axes of the slice: x: 4, y: 4, z: 8, core: 2. Of those that a mesh axis runs over, the one named last changes fastest.
Arguments:
- rhs_leaf: bfloat16 [2048, 256, 256], P(('gz', 'row', 'col')), may hold values from -6 to 6
- inv_leaf: bfloat16 [2048, 256, 256], P(('gz', 'row', 'col')), may hold values from -1 to 1.5, as said below
- couple_leaf: bfloat16 [2048, 1536, 256], P(('gz', 'row', 'col')), may hold values from -0.0625 to 0.0625
- pattern: int32 [2048, 12], P(('gz', 'row', 'col')), may hold values 0 or 1
- rhs_grid: bfloat16 [16, 1536, 256], P('gz', 'col'), may hold values from -6 to 6
- inv_grid: bfloat16 [16, 1536, 1536], P('gz', 'row', 'col'), may hold values from -1 to 1.5, as said below
- couple_grid: bfloat16 [16, 1024, 1536], P('gz', 'col', 'row'), may hold values from -0.0390625 to 0.0390625
- rhs_root: bfloat16 [1024, 256], P('col'), may hold values from -6 to 6
- inv_root: bfloat16 [1024, 1024], P('row', 'col'), may hold values from -1 to 1.5, as said below
Outputs:
- solve_leaf: float32 [2048, 256, 256], P(('gz', 'row', 'col'))
- solve_grid: float32 [16, 1536, 256], P('gz', 'col')
- solve_root: float32 [1024, 256], P('col')
The draws below stay inside these ranges and needn't reach their ends.
Inputs may be any that keep to these rules, and one draw needn't show every extreme that they name: `inv_leaf`: each 256 x 256 block is lower triangular with a diagonal between 0.5 and 1.5. `inv_grid`: each 1536 x 1536 block is lower triangular with a diagonal between 0.5 and 1.5. `inv_root`: lower triangular with a diagonal between 0.5 and 1.5.
All inputs are finite; a program needn't handle non-finite values. No bound on the sum of `pattern` on one device may be relied on, other than what follows from the above.
Results may differ from the reference program's by a relative error of at most 0.0075.
Values may be sent and summed in bfloat16 or wider, within the bound.
A program may use at most 64 MiB of HBM per device.

```python
import math
import jax
import jax.numpy as jnp
from jax import lax

NRHS = 256
BLK = 128
SN = 256
SG = 1536
SR = 1024
GRIDS = 16
LEAVES = 2048


def lower_block(lower_part, diagonal_part, order):
    rows_index = lax.broadcasted_iota(jnp.int32, (order, order), 0)
    cols_index = lax.broadcasted_iota(jnp.int32, (order, order), 1)
    below = (rows_index > cols_index).astype(jnp.float32)
    same = (rows_index == cols_index).astype(jnp.float32)
    return lower_part * below * (0.5 / math.sqrt(order)) + diagonal_part[..., None] * same


def draw_inv_leaf(key, part):
    key = jax.random.fold_in(key, 5)
    first_key, second_key = jax.random.split(key)
    layout = (LEAVES, SN, SN)
    lower_part = jnp.clip(jax.random.normal(first_key, layout, jnp.float32), -5.0, 5.0)
    diagonal_part = jax.random.uniform(second_key, layout[:-1], jnp.float32, 0.7, 1.3)
    return lower_block(lower_part, diagonal_part, SN).astype(jnp.bfloat16)


def draw_inv_grid(key, part):
    key = jax.random.fold_in(key, 7)
    first_key, second_key = jax.random.split(key)
    layout = (GRIDS, SG, SG)
    lower_part = jnp.clip(jax.random.normal(first_key, layout, jnp.float32), -5.0, 5.0)
    diagonal_part = jax.random.uniform(second_key, layout[:-1], jnp.float32, 0.7, 1.3)
    return lower_block(lower_part, diagonal_part, SG).astype(jnp.bfloat16)


def draw_inv_root(key, part):
    key = jax.random.fold_in(key, 9)
    first_key, second_key = jax.random.split(key)
    layout = (SR, SR)
    lower_part = jnp.clip(jax.random.normal(first_key, layout, jnp.float32), -5.0, 5.0)
    diagonal_part = jax.random.uniform(second_key, layout[:-1], jnp.float32, 0.7, 1.3)
    return lower_block(lower_part, diagonal_part, SR).astype(jnp.bfloat16)


def place_ends(entries, key, low, largest):
    extent = entries.shape
    spot = [jax.random.randint(jax.random.fold_in(key, axis), (), 0, extent[axis]) for axis in range(len(extent))]
    entries = entries.at[tuple(spot)].set(low)
    longest = extent.index(max(extent))
    spot[longest] = (spot[longest] + 1) % extent[longest]
    return entries.at[tuple(spot)].set(largest)


def level_of(rng, shape, cuts, low, largest):
    def one(dim, parts):
        heights = jax.random.uniform(jax.random.fold_in(jax.random.fold_in(rng, 6), dim), (parts,), jnp.float32, low / len(cuts), largest / len(cuts))
        return jnp.repeat(jnp.exp(heights), shape[dim] // parts).reshape((-1,) + (1,) * (len(shape) - dim - 1))

    loudness = one(*cuts[0])
    for cut in cuts[1:]:
        loudness = loudness * one(*cut)
    return loudness


def centred(rng, dims, deviation, most, cuts=(), dtype=jnp.bfloat16):
    level = level_of(rng, dims, cuts, -0.22, 0.18) if cuts else 1.0
    entries = jax.random.normal(rng, dims, jnp.float32) * deviation * level
    return jnp.minimum(jnp.maximum(entries, -most), most).astype(dtype)


def setup_inputs(seed: int = 0) -> dict:
    seeds = jax.random.split(jax.random.key(seed), 10)
    return {
        "rhs_leaf": centred(seeds[0], (LEAVES, SN, NRHS), 1.0, 6.0, ((0, 256),)),
        "inv_leaf": draw_inv_leaf(jax.random.fold_in(seeds[9], 71), 0),
        "couple_leaf": centred(seeds[2], (LEAVES, SG, SN), (32 * SN) ** -0.5, 0.0625, ((0, 256),)),
        "pattern": place_ends((jax.random.randint(seeds[3], (LEAVES, SG // BLK), 0, 2) < 1).astype(jnp.int32), jax.random.fold_in(seeds[3], 1), 0, 1),
        "rhs_grid": centred(seeds[4], (GRIDS, SG, NRHS), 1.0, 6.0, ((0, 16), (1, 4))),
        "inv_grid": draw_inv_grid(jax.random.fold_in(seeds[9], 71), 0),
        "couple_grid": centred(seeds[6], (GRIDS, SR, SG), (16 * SG) ** -0.5, 0.0390625, ((0, 16), (1, 4), (2, 4))),
        "rhs_root": centred(seeds[7], (SR, NRHS), 1.0, 6.0, ((0, 4),)),
        "inv_root": draw_inv_root(jax.random.fold_in(seeds[9], 71), 0),
    }


def row_mask(pattern_rows):
    return jnp.repeat(pattern_rows, BLK, axis=1).astype(jnp.float32)


def rounded(values):
    return lax.optimization_barrier(values.astype(jnp.bfloat16))


def reference(rhs_leaf, inv_leaf, couple_leaf, pattern, rhs_grid, inv_grid, couple_grid, rhs_root, inv_root):
    per_grid = LEAVES // GRIDS

    def group(array):
        return array.reshape((GRIDS, per_grid) + array.shape[1:])

    def forward_grid(operands):
        leaf_rhs, leaf_inv, leaf_couple, leaf_pattern, grid_rhs, grid_inv = operands
        leaf_sol = rounded(jnp.einsum('lij,ljk->lik', leaf_inv.astype(jnp.float32), leaf_rhs.astype(jnp.float32)))
        masked = leaf_couple.astype(jnp.float32) * row_mask(leaf_pattern)[:, :, None]
        update = jnp.einsum('lgj,ljk->gk', masked, leaf_sol.astype(jnp.float32))
        grid_res = rounded(grid_rhs.astype(jnp.float32) - update)
        grid_sol = rounded(jnp.dot(grid_inv, grid_res, preferred_element_type=jnp.float32))
        return leaf_sol, grid_sol

    leaf_fwd, grid_fwd = lax.map(forward_grid, (group(rhs_leaf), group(inv_leaf), group(couple_leaf), group(pattern), rhs_grid, inv_grid))
    root_update = jnp.einsum('gij,gjk->ik', couple_grid.astype(jnp.float32), grid_fwd.astype(jnp.float32))
    root_res = rounded(rhs_root.astype(jnp.float32) - root_update)
    root_fwd = rounded(jnp.dot(inv_root, root_res, preferred_element_type=jnp.float32))
    solve_root = jnp.dot(inv_root.T, root_fwd, preferred_element_type=jnp.float32)
    root_half = rounded(solve_root)

    def backward_grid(operands):
        leaf_sol, leaf_inv, leaf_couple, leaf_pattern, grid_sol, grid_inv, grid_couple = operands
        correction = jnp.dot(grid_couple.T, root_half, preferred_element_type=jnp.float32)
        grid_res = rounded(grid_sol.astype(jnp.float32) - correction)
        grid_out = jnp.dot(grid_inv.T, grid_res, preferred_element_type=jnp.float32)
        grid_half = rounded(grid_out)
        masked = leaf_couple.astype(jnp.float32) * row_mask(leaf_pattern)[:, :, None]
        leaf_update = jnp.einsum('lgj,gk->ljk', masked, grid_half.astype(jnp.float32))
        leaf_res = rounded(leaf_sol.astype(jnp.float32) - leaf_update)
        leaf_out = jnp.einsum('lji,ljk->lik', leaf_inv.astype(jnp.float32), leaf_res.astype(jnp.float32))
        return leaf_out, grid_out

    leaf_out, grid_out = lax.map(backward_grid, (leaf_fwd, group(inv_leaf), group(couple_leaf), group(pattern), grid_fwd, inv_grid, couple_grid))
    return leaf_out.reshape(LEAVES, SN, NRHS), grid_out, solve_root
```

```python
import jax
import jax.numpy as jnp
from jax import lax
from jax.experimental import pallas as pl
from jax.experimental.pallas import tpu as pltpu
from jax.sharding import PartitionSpec as P

MESH = pl.DeviceIdType.MESH
F32 = jnp.float32
BF16 = jnp.bfloat16

NL = 8
N = 256
GB = 384
GP = 96
SG = 1536
RB = 256
NRHS = 256
SLICE = 16


def dot(a, b):
    return jnp.dot(a, b, preferred_element_type=F32)


def dot_nt(a, b):
    return lax.dot_general(a, b, (((1,), (1,)), ((), ())), preferred_element_type=F32)


def kernel(
    rhs_leaf, inv_leaf, couple_leaf, pattern, rhs_grid, inv_grid, couple_grid, rhs_root, inv_root,
    out_leaf, out_grid, out_root,
    rl, il, cl, fl, ct, ilt, ol,
    own1, snd1, rcv1, rg, part, psnd, rcv3, fg, coupleT, gridT,
    ut, usnd, rcv4, rootT_rhs, rcv5, wsnd, blocks, rr, rt, hsnd,
    csnd, rcv7, gb, qsnd, rcv8, xg,
    in_sems, leaf_sems, c_sems, out_sems, blk_sem,
    s1, r1, s2, r2, s3, r3, s3b, r3b, s4, r4, s5, r5, s6, r6, s7, r7, s7b, r7b, s8, r8, s9, r9,
    sR, rR, sC, rC,
):
    gz = lax.axis_index("gz")
    x = lax.axis_index("row")
    y = lax.axis_index("col")
    core = lax.rem(gz, 2)
    sibling = gz + 1 - 2 * core
    here = x * 4 + y

    def xpart(k):
        return (gz, lax.rem(x + k, 4), y)

    def ypart(k):
        return (gz, x, lax.rem(y + k, 4))

    def gpart(k):
        return (lax.rem(gz + k, 16), x, y)

    def ppart(k):
        return (gz, lax.rem(x + k // 4, 4), lax.rem(y + k % 4, 4))

    def remote(src, dst, ssem, rsem, dev):
        return pltpu.make_async_remote_copy(
            src_ref=src, dst_ref=dst, send_sem=ssem, recv_sem=rsem, device_id=dev, device_id_type=MESH
        )

    def rows(i, n):
        return pl.ds(pl.multiple_of(i * n, n), n)

    barrier = pltpu.get_barrier_semaphore()
    for k in range(1, 16):
        pl.semaphore_signal(barrier, inc=1, device_id=ppart(k), device_id_type=MESH)
        pl.semaphore_signal(barrier, inc=1, device_id=gpart(k), device_id_type=MESH)

    leaf_in = [
        pltpu.make_async_copy(rhs_leaf, rl, leaf_sems.at[0]),
        pltpu.make_async_copy(inv_leaf, il, leaf_sems.at[1]),
    ]
    for c in leaf_in:
        c.start()
    c_in = []
    for jj in range(4):
        block = rows(lax.rem(y + jj, 4), GB)
        c_in.append(pltpu.make_async_copy(couple_leaf.at[:, block], cl.at[:, block], c_sems.at[jj]))
        c_in[-1].start()
    half = pl.ds(pl.multiple_of(core * 128, 128), 128)
    own_block = pltpu.make_async_copy(inv_root.at[half], blocks.at[here, half], blk_sem)
    own_block.start()
    for c in leaf_in:
        c.wait()

    def leaf_fwd(l, carry):
        fl[rows(l, N), :] = dot(il[l], rl[l]).astype(BF16)
        return carry

    lax.fori_loop(0, NL, leaf_fwd, 0)
    pl.semaphore_wait(barrier, 30)

    sends = []
    for jj in range(4):
        b = lax.rem(y + jj, 4)
        c_in[jj].wait()
        parts = []
        for t in range(3):
            blk = pl.ds(pl.multiple_of(b * GB + t * 128, 128), 128)
            for l in range(NL):
                keep = pattern[l, b * 3 + t].astype(F32).astype(BF16)
                cl[l, blk, :] = cl[l, blk, :] * keep
        rb = rows(b, GB)
        acc = dot(jnp.concatenate([cl[l, rb, :] for l in range(NL)], axis=1), fl[...])
        if jj == 0:
            own1[...] = acc
        snd1[rows(jj, GB), :] = acc.astype(BF16)
        for dx in range(4):
            k = dx * 4 + jj
            if k == 0:
                continue
            piece = pl.ds(pl.multiple_of(jj * GB + lax.rem(x + dx, 4) * GP, 32), GP)
            c = remote(snd1.at[piece], rcv1.at[k], s1.at[k], r1.at[k], ppart(k))
            c.start()
            sends.append((k, c))

    own_block.wait()
    rsend = [
        remote(blocks.at[here, half], blocks.at[here, half], sR.at[k], rR.at[k], ppart(k))
        for k in range(1, 16)
    ]

    @pl.when(x >= y)
    def _():
        for c in rsend:
            c.start()

    def leaf_transpose(l, carry):
        ct[l] = cl[l].T
        ilt[l] = il[l].T
        return carry

    lax.fori_loop(0, NL, leaf_transpose, 0)
    coupleT[...] = couple_grid[0].T
    gridT[...] = inv_grid[0].T
    rootT_rhs[...] = rhs_root[...].astype(F32).T

    my_piece = rows(x, GP)
    tot = own1[my_piece, :]
    for k, c in sends:
        c.wait_recv()
    for k, c in sends:
        tot = tot + rcv1[k].astype(F32)
    rg[my_piece, :] = (rhs_grid[0, my_piece, :].astype(F32) - tot).astype(BF16)

    a2 = [remote(rg.at[my_piece], rg.at[my_piece], s2.at[k], r2.at[k], xpart(k)) for k in range(1, 4)]
    for c in a2:
        c.start()
    for c in a2:
        c.wait_recv()

    def reduce_y(partial, snd, rcv, ss, rs):
        part[...] = partial
        snd[...] = partial.astype(BF16)
        cs = [
            remote(snd.at[rows(lax.rem(y + k, 4), GP)], rcv.at[k], ss.at[k], rs.at[k], ypart(k))
            for k in range(1, 4)
        ]
        for c in cs:
            c.start()
        for c in cs:
            c.wait_recv()
        total = part[rows(y, GP), :]
        for k in range(1, 4):
            total = total + rcv[k].astype(F32)
        return total, cs

    def gather_y(buf, ss, rs):
        mine = rows(y, GP)
        cs = [remote(buf.at[mine], buf.at[mine], ss.at[k], rs.at[k], ypart(k)) for k in range(1, 4)]
        for c in cs:
            c.start()
        for c in cs:
            c.wait_recv()
        return cs

    total, a3 = reduce_y(dot(inv_grid[0], rg[...]), psnd, rcv3, s3, r3)
    fg[rows(y, GP), :] = total.astype(BF16)
    a3b = gather_y(fg, s3b, r3b)

    up = dot(couple_grid[0], fg[...]).T
    ut[...] = up
    usnd[...] = up.astype(BF16)
    a4 = [
        remote(usnd.at[rows(lax.rem(gz + k, 16), SLICE)], rcv4.at[k], s4.at[k], r4.at[k], gpart(k))
        for k in range(1, 16)
    ]
    for c in a4:
        c.start()

    for k in range(1, 16):
        @pl.when(lax.rem(x - k // 4 + 4, 4) >= lax.rem(y - k % 4 + 4, 4))
        def _():
            rsend[k - 1].wait_recv()
    pass_on = remote(blocks.at[:, half], blocks.at[:, half], sC.at[0], rC.at[0], (sibling, x, y))
    pass_on.start()

    for c in a4:
        c.wait_recv()
    mine = rows(gz, SLICE)
    v = ut[mine, :]
    for k in range(1, 16):
        v = v + rcv4[k].astype(F32)
    w = (jnp.where(x == 0, rootT_rhs[mine, :], 0.0) - v).astype(BF16)
    wsnd[...] = w
    rcv5[here] = w
    a5 = [remote(wsnd, rcv5.at[here], s5.at[k], r5.at[k], ppart(k)) for k in range(1, 16)]
    for c in a5:
        c.start()
    pass_on.wait_recv()
    for c in a5:
        c.wait_recv()
    res = []
    for j in range(4):
        t = rcv5[j].astype(F32)
        for i in range(1, 4):
            t = t + rcv5[i * 4 + j].astype(F32)
        res.append(t.astype(BF16))
    zs = []
    for i in range(4):
        t = dot_nt(res[0], blocks[i * 4])
        for j in range(1, i + 1):
            t = t + dot_nt(res[j], blocks[i * 4 + j])
        zs.append(t.astype(BF16))
    for j in range(4):
        t = dot(zs[j], blocks[j * 4 + j])
        for i in range(j + 1, 4):
            t = t + dot(zs[i], blocks[i * 4 + j])
        rr[j] = t.astype(BF16)
    hsnd[...] = rr[y]
    rt[mine, :] = rr[y]
    a6 = [remote(hsnd, rt.at[mine], s6.at[k], r6.at[k], gpart(k)) for k in range(1, 16)]
    for c in a6:
        c.start()
    for c in a6:
        c.wait_recv()
    root = rt[...].astype(F32).T
    out_root[...] = root

    total, a7 = reduce_y(dot(coupleT[...], root.astype(BF16)), csnd, rcv7, s7, r7)
    gb[rows(y, GP), :] = (fg[rows(y, GP), :].astype(F32) - total).astype(BF16)
    a7b = gather_y(gb, s7b, r7b)

    q = dot(gridT[...], gb[...])
    part[...] = q
    qsnd[...] = q.astype(BF16)
    a8 = [
        remote(qsnd.at[rows(lax.rem(x + k, 4), GP)], rcv8.at[k], s8.at[k], r8.at[k], xpart(k))
        for k in range(1, 4)
    ]
    for c in a8:
        c.start()
    for c in a8:
        c.wait_recv()
    total = part[my_piece, :]
    for k in range(1, 4):
        total = total + rcv8[k].astype(F32)
    home = rows(y * 4 + x, GP)
    xg[home, :] = total.astype(BF16)
    a9 = [remote(xg.at[home], xg.at[home], s9.at[k], r9.at[k], ppart(k)) for k in range(1, 16)]
    for c in a9:
        c.start()
    for c in a9:
        c.wait_recv()
    out_grid[0] = xg[rows(y, GB), :].astype(F32)

    for l in range(NL):
        back = (fl[l * N:(l + 1) * N, :].astype(F32) - dot(ct[l], xg[...])).astype(BF16)
        ol[l] = dot(ilt[l], back)
        pltpu.make_async_copy(ol.at[l], out_leaf.at[l], out_sems.at[l]).start()

    for k, c in sends:
        c.wait_send()

    @pl.when(x >= y)
    def _():
        for c in rsend:
            c.wait_send()

    for c in a2 + a3 + a3b + a4 + [pass_on] + a5 + a6 + a7 + a7b + a8 + a9:
        c.wait_send()
    for l in range(NL):
        pltpu.make_async_copy(ol.at[l], out_leaf.at[l], out_sems.at[l]).wait()


def on_device(*args):
    vm = pltpu.VMEM
    dma = pltpu.SemaphoreType.DMA
    vmem = pl.BlockSpec(memory_space=pltpu.VMEM)
    hbm = pl.BlockSpec(memory_space=pl.ANY)
    smem = pl.BlockSpec(memory_space=pltpu.SMEM)
    return pl.pallas_call(
        kernel,
        out_shape=(
            jax.ShapeDtypeStruct((NL, N, NRHS), F32),
            jax.ShapeDtypeStruct((1, GB, NRHS), F32),
            jax.ShapeDtypeStruct((RB, NRHS), F32),
        ),
        in_specs=[hbm, hbm, hbm, smem, vmem, vmem, vmem, vmem, hbm],
        out_specs=(hbm, vmem, vmem),
        scratch_shapes=[
            vm((NL, N, NRHS), BF16), vm((NL, N, N), BF16), vm((NL, SG, N), BF16),
            vm((NL * N, NRHS), BF16), vm((NL, N, SG), BF16), vm((NL, N, N), BF16),
            vm((NL, N, NRHS), F32),
            vm((GB, NRHS), F32), vm((SG, NRHS), BF16), vm((16, GP, NRHS), BF16),
            vm((GB, NRHS), BF16), vm((GB, NRHS), F32), vm((GB, NRHS), BF16),
            vm((4, GP, NRHS), BF16), vm((GB, NRHS), BF16), vm((GB, RB), BF16), vm((GB, GB), BF16),
            vm((NRHS, RB), F32), vm((NRHS, RB), BF16), vm((16, SLICE, RB), BF16),
            vm((NRHS, RB), F32), vm((16, SLICE, RB), BF16), vm((SLICE, RB), BF16),
            vm((16, RB, RB), BF16), vm((4, SLICE, RB), BF16), vm((NRHS, RB), BF16),
            vm((SLICE, RB), BF16),
            vm((GB, NRHS), BF16), vm((4, GP, NRHS), BF16), vm((GB, NRHS), BF16),
            vm((GB, NRHS), BF16), vm((4, GP, NRHS), BF16), vm((SG, NRHS), BF16),
            dma((8,)), dma((2,)), dma((4,)), dma((8,)), dma(()),
            dma((16,)), dma((16,)), dma((4,)), dma((4,)), dma((4,)), dma((4,)), dma((4,)), dma((4,)),
            dma((16,)), dma((16,)), dma((16,)), dma((16,)), dma((16,)), dma((16,)),
            dma((4,)), dma((4,)), dma((4,)), dma((4,)), dma((4,)), dma((4,)), dma((16,)), dma((16,)),
            dma((16,)), dma((16,)), dma((1,)), dma((1,)),
        ],
        compiler_params=pltpu.CompilerParams(
            collective_id=0, has_side_effects=True, vmem_limit_bytes=48 << 20
        ),
        cost_estimate=pl.CostEstimate(flops=4_200_000_000, bytes_accessed=13_000_000, transcendentals=0),
        name="solve",
    )(*args)


def solution(mesh):
    return jax.shard_map(
        on_device,
        mesh=mesh,
        in_specs=(
            P(("gz", "row", "col"), None, None),
            P(("gz", "row", "col"), None, None),
            P(("gz", "row", "col"), None, None),
            P(("gz", "row", "col"), None),
            P("gz", "col", None),
            P("gz", "row", "col"),
            P("gz", "col", "row"),
            P("col", None),
            P("row", "col"),
        ),
        out_specs=(P(("gz", "row", "col"), None, None), P("gz", "col", None), P("col", None)),
        check_vma=False,
    )
```

```python
import jax
import jax.numpy as jnp
from jax import lax
from jax.experimental import pallas as pl
from jax.experimental.pallas import tpu as pltpu
from jax.sharding import PartitionSpec as P

MESH = pl.DeviceIdType.MESH
F32 = jnp.float32
BF16 = jnp.bfloat16

NL = 8
N = 256
GB = 384
GP = 96
SG = 1536
RB = 256
NRHS = 256
HALF = SG // 2
SLICE = 16


def dot(a, b):
    return jnp.dot(a, b, preferred_element_type=F32)


def dot_nt(a, b):
    return lax.dot_general(a, b, (((1,), (1,)), ((), ())), preferred_element_type=F32)


def dot_tn(a, b):
    return lax.dot_general(a, b, (((0,), (0,)), ((), ())), preferred_element_type=F32)


def kernel(
    rhs_leaf, inv_leaf, couple_leaf, pattern, rhs_grid, inv_grid, couple_grid, rhs_root, inv_root,
    out_back, out_top, out_root,
    rl, il, cl, fl, ct, ol, back, xg, lg, rgrid, rroot,
    cg, bsnd, rcvb, bacc, bm, btm, bts,
    own1, snd1, rcv1, rg, part, psnd, rcv3, fg, gridT, hpart, hsnd, rcv8,
    ut, usnd, rcv4, rootT_rhs, rcv5, wsnd, blocks, rt,
    in_sems, c_sems, out_sems,
    s1, r1, s2, r2, s3, r3, s3b, r3b, s4, r4, s5, r5, s6, r6, s8, r8, s9, r9,
    sR, rR, sC, rC, sG, rG, sB, rB, sT, rT,
):
    gz = lax.axis_index("gz")
    x = lax.axis_index("row")
    y = lax.axis_index("col")
    core = lax.rem(gz, 2)
    sibling = (gz + 1 - 2 * core, x, y)
    here = x * 4 + y

    def xpart(k):
        return (gz, lax.rem(x + k, 4), y)

    def ypart(k):
        return (gz, x, lax.rem(y + k, 4))

    def gpart(k):
        return (lax.rem(gz + k, 16), x, y)

    def ppart(k):
        return (gz, lax.rem(x + k // 4, 4), lax.rem(y + k % 4, 4))

    def remote(src, dst, ssem, rsem, dev):
        return pltpu.make_async_remote_copy(
            src_ref=src, dst_ref=dst, send_sem=ssem, recv_sem=rsem, device_id=dev, device_id_type=MESH
        )

    def rows(i, n):
        return pl.ds(pl.multiple_of(i * n, n), n)

    pending = []

    def start(copies, when=None):
        for c in copies:
            if when is None:
                c.start()
            else:
                pl.when(when)(c.start)
            pending.append((c, when))

    def arrived(copies, when=None):
        for c in copies:
            if when is None:
                c.wait_recv()
            else:
                pl.when(when)(c.wait_recv)

    def finish():
        for c, when in pending:
            if when is None:
                c.wait_send()
            else:
                pl.when(when)(c.wait_send)

    mine = rows(gz, SLICE)
    mine_root = x * (x + 1) // 2 + y
    load_r = pltpu.make_async_copy(rhs_leaf, rl, in_sems.at[0])
    load_i = pltpu.make_async_copy(inv_leaf, il, in_sems.at[1])
    load_r.start()
    load_i.start()
    load_c = []
    for jj in range(4):
        block = rows(lax.rem(y + jj, 4), GB)
        load_c.append(pltpu.make_async_copy(couple_leaf.at[:, block], cl.at[:, block], c_sems.at[jj]))
        load_c[-1].start()
    loads = [
        pltpu.make_async_copy(couple_grid.at[0], cg.at[y], in_sems.at[2]),
        pltpu.make_async_copy(inv_grid.at[0], lg, in_sems.at[3]),
        pltpu.make_async_copy(rhs_grid.at[0], rgrid, in_sems.at[4]),
        pltpu.make_async_copy(rhs_root, rroot, in_sems.at[5]),
    ]
    for c in loads:
        c.start()
    load_b = pltpu.make_async_copy(inv_root.at[mine], blocks.at[mine_root, mine], in_sems.at[6])
    pl.when(x >= y)(load_b.start)

    barrier = pltpu.get_barrier_semaphore()
    for k in range(1, 16):
        pl.semaphore_signal(barrier, inc=1, device_id=ppart(k), device_id_type=MESH)
        pl.semaphore_signal(barrier, inc=1, device_id=gpart(k), device_id_type=MESH)

    load_r.wait()
    load_i.wait()

    for l in range(NL):
        fl[l * N:(l + 1) * N, :] = dot(il[l], rl[l]).astype(BF16)

    a1 = []
    for jj in range(4):
        b = lax.rem(y + jj, 4)
        load_c[jj].wait()
        for t in range(3):
            blk = pl.ds(pl.multiple_of(b * GB + t * 128, 128), 128)
            for l in range(NL):
                keep = pattern[l, b * 3 + t].astype(F32).astype(BF16)
                cl[l, blk, :] = cl[l, blk, :] * keep
        rb = rows(b, GB)
        acc = dot(jnp.concatenate([cl[l, rb, :] for l in range(NL)], axis=1), fl[...])
        if jj == 0:
            own1[...] = acc
        snd1[rows(jj, GB), :] = acc.astype(BF16)
        if jj == 1:
            pl.semaphore_wait(barrier, 30)
        for sent in {0: (), 1: (0, 1), 2: (2,), 3: (3,)}[jj]:
            for dx in range(4):
                k = dx * 4 + sent
                if k == 0:
                    continue
                piece = pl.ds(pl.multiple_of(sent * GB + lax.rem(x + dx, 4) * GP, 32), GP)
                a1.append(remote(snd1.at[piece], rcv1.at[k], s1.at[k], r1.at[k], ppart(k)))
                start(a1[-1:])

    pl.when(x >= y)(load_b.wait)
    rsend = [
        remote(blocks.at[mine_root, mine], blocks.at[mine_root, mine], sR.at[k], rR.at[k], ppart(k))
        for k in range(1, 16)
    ]
    start(rsend, x >= y)

    def leaf_transpose(l, carry):
        ct[l] = cl[l].T
        return carry

    lax.fori_loop(0, 2, leaf_transpose, 0)
    for c in loads:
        c.wait()
    gridT[...] = lg[...].T
    rootT_rhs[...] = rroot[...].astype(F32).T
    for k in range(1, 16):
        arrived([rsend[k - 1]], lax.rem(x - k // 4 + 4, 4) >= lax.rem(y - k % 4 + 4, 4))
    zsend = [
        remote(blocks.at[:, mine], blocks.at[:, mine], sC.at[k], rC.at[k], gpart(k)) for k in range(2, 16, 2)
    ]
    zpass = [remote(blocks.at[:, mine], blocks.at[:, mine], sC.at[1], rC.at[1], sibling)]
    start(zsend)
    start(zpass)
    my_piece = rows(x, GP)
    arrived(a1)
    tot = own1[my_piece, :]
    for k in range(1, 16):
        tot = tot + rcv1[k].astype(F32)
    rg[my_piece, :] = (rgrid[my_piece, :].astype(F32) - tot).astype(BF16)

    a2 = [remote(rg.at[my_piece], rg.at[my_piece], s2.at[k], r2.at[k], xpart(k)) for k in range(1, 4)]
    start(a2)
    lax.fori_loop(2, 4, leaf_transpose, 0)
    arrived(a2)
    partial = dot(lg[...], rg[...])
    part[...] = partial
    psnd[...] = partial.astype(BF16)
    a3 = [
        remote(psnd.at[rows(lax.rem(y + k, 4), GP)], rcv3.at[k], s3.at[k], r3.at[k], ypart(k))
        for k in range(1, 4)
    ]
    start(a3)
    lax.fori_loop(4, 6, leaf_transpose, 0)
    my_rows = rows(y, GP)
    arrived(a3)
    total = part[my_rows, :]
    for k in range(1, 4):
        total = total + rcv3[k].astype(F32)
    fg[my_rows, :] = total.astype(BF16)
    a3b = [remote(fg.at[my_rows], fg.at[my_rows], s3b.at[k], r3b.at[k], ypart(k)) for k in range(1, 4)]
    start(a3b)
    gsend = [remote(couple_grid.at[0], cg.at[y], sG.at[k], rG.at[k], ypart(k)) for k in range(1, 4)]

    for k in range(1, 4):
        start([gsend[k - 1]], lax.rem(y + k, 4) <= x)
    lax.fori_loop(6, 8, leaf_transpose, 0)
    arrived(a3b)
    up = dot(cg[y], fg[...]).T
    ut[...] = up
    usnd[...] = up.astype(BF16)
    a4 = [
        remote(usnd.at[rows(lax.rem(gz + k, 16), SLICE)], rcv4.at[k], s4.at[k], r4.at[k], gpart(k))
        for k in range(1, 16)
    ]
    start(a4)
    partial = dot(gridT[...], fg[...])
    hpart[...] = partial
    hsnd[...] = partial.astype(BF16)
    a8 = [
        remote(hsnd.at[rows(lax.rem(x + k, 4), GP)], rcv8.at[k], s8.at[k], r8.at[k], xpart(k))
        for k in range(1, 4)
    ]
    start(a8)
    for i, k in enumerate(range(2, 16, 2)):
        arrived([zsend[i]])
        from_z = rows(lax.rem(gz - k + 16, 16), SLICE)
        zpass.append(remote(blocks.at[:, from_z], blocks.at[:, from_z], sC.at[k + 1], rC.at[k + 1], sibling))
        start(zpass[-1:])
    arrived(gsend, y <= x)

    @pl.when(y <= x)
    def _():
        for a in range(4):
            bsnd[a] = dot(cg[a], lg[...]).astype(BF16)

    bsend = [
        remote(bsnd.at[lax.rem(x + k, 4)], rcvb.at[k], sB.at[k], rB.at[k], xpart(k)) for k in range(1, 4)
    ]
    start(bsend, y <= x)
    arrived(a4)
    v = ut[mine, :]
    for k in range(1, 16):
        v = v + rcv4[k].astype(F32)
    w = (jnp.where(x == 0, rootT_rhs[mine, :], 0.0) - v).astype(BF16)
    wsnd[...] = w
    rcv5[here] = w
    a5 = [remote(wsnd, rcv5.at[here], s5.at[k], r5.at[k], ppart(k)) for k in range(1, 16)]
    start(a5)
    arrived(a8)
    hpart[my_piece, :] += rcv8[1].astype(F32) + rcv8[2].astype(F32) + rcv8[3].astype(F32)
    arrived(zpass)
    arrived(a5)
    res = []
    for j in range(4):
        t = rcv5[j].astype(F32)
        for i in range(1, 4):
            t = t + rcv5[i * 4 + j].astype(F32)
        res.append(t.astype(BF16))
    zs = []
    for i in range(4):
        t = dot_nt(res[0], blocks[i * (i + 1) // 2])
        for j in range(1, i + 1):
            t = t + dot_nt(res[j], blocks[i * (i + 1) // 2 + j])
        zs.append(t.astype(BF16))
    for j in range(4):
        t = dot(zs[j], blocks[j * (j + 1) // 2 + j])
        for i in range(j + 1, 4):
            t = t + dot(zs[i], blocks[i * (i + 1) // 2 + j])
        rt[mine, j * RB:(j + 1) * RB] = t.astype(BF16)

    a6 = [remote(rt.at[mine], rt.at[mine], s6.at[k], r6.at[k], gpart(k)) for k in range(2, 16, 2)]
    start(a6)
    a6b = [remote(rt.at[mine], rt.at[mine], s6.at[1], r6.at[1], sibling)]
    start(a6b)
    bacc[...] = jnp.zeros_like(bacc)

    @pl.when(y <= x)
    def _():
        bacc[...] = bsnd[x].astype(F32)

    for k in range(1, 4):
        sent = lax.rem(x - k + 4, 4) >= y
        arrived([bsend[k - 1]], sent)

        @pl.when(sent)
        def _():
            bacc[...] += rcvb[k].astype(F32)

    bm[...] = bacc[...].astype(BF16)
    btm[...] = bm[...].T
    bts[x] = btm[my_piece, :]
    at = [
        remote(btm.at[rows(lax.rem(x + k, 4), GP)], bts.at[x], sT.at[k], rT.at[k], xpart(k))
        for k in range(1, 4)
    ]
    start(at)
    for i, k in enumerate(range(2, 16, 2)):
        arrived([a6[i]])
        from_z = rows(lax.rem(gz - k + 16, 16), SLICE)
        a6b.append(
            remote(rt.at[from_z], rt.at[from_z], s6.at[k + 1], r6.at[k + 1], sibling)
        )
        start(a6b[-1:])
    arrived(at)
    arrived(a6b)
    h = hpart[my_piece, :]
    for i in range(4):
        h = h - dot_nt(bts[i], rt[:, i * RB:(i + 1) * RB])
    home = rows(y * 4 + x, GP)
    xg[home, :] = h.astype(BF16)
    a9 = [remote(xg.at[home], xg.at[home], s9.at[k], r9.at[k], ppart(k)) for k in range(1, 16)]
    start(a9)
    stores = [pltpu.make_async_copy(rt.at[:, rows(y, RB)], out_root, out_sems.at[2])]
    stores[0].start()
    odd = lax.rem(y, 2) == 1
    for k in range(1, 16):
        dy = k % 4
        if dy == 0:
            arrived(a9[k - 1:k])
        elif dy == 1:
            arrived(a9[k - 1:k], odd)
        elif dy == 3:
            arrived(a9[k - 1:k], jnp.logical_not(odd))
    top = pl.ds(pl.multiple_of((y // 2) * HALF, HALF), HALF)
    for g in range(2):
        ls = slice(g * 4, g * 4 + 4)
        t = dot(ct[ls, :, top].reshape(4 * N, HALF), xg[top, :])
        gs = slice(g * 4 * N, (g + 1) * 4 * N)
        ol[gs, :] = fl[gs, :].astype(F32) - t
    for k in range(1, 16):
        dy = k % 4
        if dy == 2:
            arrived(a9[k - 1:k])
        elif dy == 1:
            arrived(a9[k - 1:k], jnp.logical_not(odd))
        elif dy == 3:
            arrived(a9[k - 1:k], odd)
    rest = pl.ds(pl.multiple_of((1 - y // 2) * HALF, HALF), HALF)
    for g in range(2):
        gs = slice(g * 4 * N, (g + 1) * 4 * N)
        t = dot(ct[g * 4:g * 4 + 4, :, rest].reshape(4 * N, HALF), xg[rest, :])
        back[gs, :] = (ol[gs, :] - t).astype(BF16)
        stores.append(pltpu.make_async_copy(back.at[gs], out_back.at[gs], out_sems.at[g]))
        stores[-1].start()
    stores.append(pltpu.make_async_copy(xg.at[rows(y, GB)], out_top, out_sems.at[3]))
    stores[-1].start()
    finish()
    for c in stores:
        c.wait()


def leaves_back(
    inv_leaf, res_leaf, top, root, out_leaf, out_grid, out_root,
    il, bk, tp, rt, sol, og, oroot, i_sems, b_sems, sems,
):
    loads = []
    for l in range(NL):
        loads.append((
            pltpu.make_async_copy(inv_leaf.at[l], il.at[l], i_sems.at[l]),
            pltpu.make_async_copy(res_leaf.at[pl.ds(l * N, N)], bk.at[l], b_sems.at[l]),
        ))
        for c in loads[l]:
            c.start()
    small = [pltpu.make_async_copy(top, tp, sems.at[NL + 2]), pltpu.make_async_copy(root, rt, sems.at[NL + 3])]
    for c in small:
        c.start()
    copies = []
    for l in range(NL):
        for c in loads[l]:
            c.wait()
        sol[l] = dot_tn(il[l], bk[l])
        copies.append(pltpu.make_async_copy(sol.at[l], out_leaf.at[l], sems.at[l]))
        copies[-1].start()
    for c in small:
        c.wait()
    og[...] = tp[...].astype(F32)
    copies.append(pltpu.make_async_copy(og, out_grid.at[0], sems.at[NL]))
    copies[-1].start()
    oroot[...] = rt[...].astype(F32).T
    copies.append(pltpu.make_async_copy(oroot, out_root, sems.at[NL + 1]))
    copies[-1].start()
    for c in copies:
        c.wait()


def on_device(*args):
    vm = pltpu.VMEM
    dma = pltpu.SemaphoreType.DMA
    hbm = pl.BlockSpec(memory_space=pl.ANY)
    smem = pl.BlockSpec(memory_space=pltpu.SMEM)
    kept = pl.pallas_call(
        kernel,
        out_shape=(
            jax.ShapeDtypeStruct((NL * N, NRHS), BF16),
            jax.ShapeDtypeStruct((GB, NRHS), BF16),
            jax.ShapeDtypeStruct((NRHS, RB), BF16),
        ),
        in_specs=[hbm, hbm, hbm, smem, hbm, hbm, hbm, hbm, hbm],
        out_specs=(hbm, hbm, hbm),
        scratch_shapes=[
            vm((NL, N, NRHS), BF16), vm((NL, N, N), BF16), vm((NL, SG, N), BF16),
            vm((NL * N, NRHS), BF16), vm((NL, N, SG), BF16), vm((NL * N, NRHS), F32),
            vm((NL * N, NRHS), BF16), vm((SG, NRHS), BF16), vm((GB, GB), BF16), vm((GB, NRHS), BF16), vm((RB, NRHS), BF16),
            vm((4, RB, GB), BF16), vm((4, RB, GB), BF16), vm((4, RB, GB), BF16), vm((RB, GB), F32),
            vm((RB, GB), BF16), vm((GB, RB), BF16), vm((4, GP, RB), BF16),
            vm((GB, NRHS), F32), vm((SG, NRHS), BF16), vm((16, GP, NRHS), BF16),
            vm((GB, NRHS), BF16), vm((GB, NRHS), F32), vm((GB, NRHS), BF16),
            vm((4, GP, NRHS), BF16), vm((GB, NRHS), BF16), vm((GB, GB), BF16),
            vm((GB, NRHS), F32), vm((GB, NRHS), BF16), vm((4, GP, NRHS), BF16),
            vm((NRHS, RB), F32), vm((NRHS, RB), BF16), vm((16, SLICE, RB), BF16),
            vm((NRHS, RB), F32), vm((16, SLICE, RB), BF16), vm((SLICE, RB), BF16),
            vm((10, RB, RB), BF16), vm((NRHS, 4 * RB), BF16),
            dma((7,)), dma((4,)), dma((4,)),
            dma((16,)), dma((16,)), dma((4,)), dma((4,)), dma((4,)), dma((4,)), dma((4,)), dma((4,)),
            dma((16,)), dma((16,)), dma((16,)), dma((16,)), dma((16,)), dma((16,)),
            dma((4,)), dma((4,)), dma((16,)), dma((16,)),
            dma((16,)), dma((16,)), dma((16,)), dma((16,)), dma((4,)), dma((4,)), dma((4,)), dma((4,)),
            dma((4,)), dma((4,)),
        ],
        compiler_params=pltpu.CompilerParams(
            collective_id=0, has_side_effects=True, vmem_limit_bytes=62 << 20
        ),
        cost_estimate=pl.CostEstimate(flops=4_200_000_000, bytes_accessed=13_000_000, transcendentals=0),
        name="solve",
    )(*args)
    return pl.pallas_call(
        leaves_back,
        out_shape=(
            jax.ShapeDtypeStruct((NL, N, NRHS), F32),
            jax.ShapeDtypeStruct((1, GB, NRHS), F32),
            jax.ShapeDtypeStruct((RB, NRHS), F32),
        ),
        in_specs=[hbm] * 4,
        out_specs=(hbm, hbm, hbm),
        scratch_shapes=[
            vm((NL, N, N), BF16), vm((NL, N, NRHS), BF16), vm((GB, NRHS), BF16), vm((NRHS, RB), BF16),
            vm((NL, N, NRHS), F32), vm((GB, NRHS), F32), vm((RB, NRHS), F32),
            dma((NL,)), dma((NL,)), dma((NL + 4,)),
        ],
        compiler_params=pltpu.CompilerParams(vmem_limit_bytes=62 << 20),
        cost_estimate=pl.CostEstimate(flops=270_000_000, bytes_accessed=4_800_000, transcendentals=0),
        name="leaves_back",
    )(args[1], *kept)


def solution(mesh):
    return jax.shard_map(
        on_device,
        mesh=mesh,
        in_specs=(
            P(("gz", "row", "col"), None, None),
            P(("gz", "row", "col"), None, None),
            P(("gz", "row", "col"), None, None),
            P(("gz", "row", "col"), None),
            P("gz", "col", None),
            P("gz", "row", "col"),
            P("gz", "col", "row"),
            P("col", None),
            P("row", "col"),
        ),
        out_specs=(P(("gz", "row", "col"), None, None), P("gz", "col", None), P("col", None)),
        check_vma=False,
    )
```

```python
import jax
import jax.numpy as jnp
from jax import lax
from jax.experimental import pallas as pl
from jax.experimental.pallas import tpu as pltpu
from jax.sharding import PartitionSpec as P

MESH = pl.DeviceIdType.MESH
F32 = jnp.float32
BF16 = jnp.bfloat16

NL = 8
N = 256
GB = 384
GP = 96
SG = 1536
RB = 256
NRHS = 256
HALF = SG // 2
SLICE = 16


def dot(a, b):
    return jnp.dot(a, b, preferred_element_type=F32)


def dot_nt(a, b):
    return lax.dot_general(a, b, (((1,), (1,)), ((), ())), preferred_element_type=F32)


def dot_tn(a, b):
    return lax.dot_general(a, b, (((0,), (0,)), ((), ())), preferred_element_type=F32)


def kernel(
    rhs_leaf, inv_leaf, couple_leaf, pattern, rhs_grid, inv_grid, couple_grid, rhs_root, inv_root,
    out_back, out_top, out_root,
    rl, il, cl, fl, ct, ol, back, xg, lg, rgrid, rroot,
    cg, bsnd, rcvb, bacc, bm, btm, bts,
    own1, snd1, rcv1, rg, part, psnd, rcv3, fg, gridT, hpart, hsnd, rcv8,
    ut, usnd, rcv4, rootT_rhs, rcv5, wsnd, blocks, rt,
    in_sems, c_sems, out_sems,
    s1, r1, s2, r2, s3, r3, s3b, r3b, s4, r4, s5, r5, s6, r6, s8, r8, s9, r9,
    sR, rR, sC, rC, sG, rG, sB, rB, sT, rT,
):
    gz = lax.axis_index("gz")
    x = lax.axis_index("row")
    y = lax.axis_index("col")
    core = lax.rem(gz, 2)
    sibling = (gz + 1 - 2 * core, x, y)
    here = x * 4 + y

    def xpart(k):
        return (gz, lax.rem(x + k, 4), y)

    def ypart(k):
        return (gz, x, lax.rem(y + k, 4))

    def gpart(k):
        return (lax.rem(gz + k, 16), x, y)

    def ppart(k):
        return (gz, lax.rem(x + k // 4, 4), lax.rem(y + k % 4, 4))

    def remote(src, dst, ssem, rsem, dev):
        return pltpu.make_async_remote_copy(
            src_ref=src, dst_ref=dst, send_sem=ssem, recv_sem=rsem, device_id=dev, device_id_type=MESH
        )

    def rows(i, n):
        return pl.ds(pl.multiple_of(i * n, n), n)

    pending = []

    def start(copies, when=None):
        for c in copies:
            if when is None:
                c.start()
            else:
                pl.when(when)(c.start)
            pending.append((c, when))

    def arrived(copies, when=None):
        for c in copies:
            if when is None:
                c.wait_recv()
            else:
                pl.when(when)(c.wait_recv)

    def finish():
        for c, when in pending:
            if when is None:
                c.wait_send()
            else:
                pl.when(when)(c.wait_send)

    mine = rows(gz, SLICE)
    mine_root = x * (x + 1) // 2 + y
    load_r = pltpu.make_async_copy(rhs_leaf, rl, in_sems.at[0])
    load_i = pltpu.make_async_copy(inv_leaf, il, in_sems.at[1])
    load_r.start()
    load_i.start()
    load_c = []
    for jj in range(4):
        block = rows(lax.rem(y + jj, 4), GB)
        load_c.append(pltpu.make_async_copy(couple_leaf.at[:, block], cl.at[:, block], c_sems.at[jj]))
        load_c[-1].start()
    loads = [
        pltpu.make_async_copy(couple_grid.at[0], cg.at[y], in_sems.at[2]),
        pltpu.make_async_copy(inv_grid.at[0], lg, in_sems.at[3]),
        pltpu.make_async_copy(rhs_grid.at[0], rgrid, in_sems.at[4]),
        pltpu.make_async_copy(rhs_root, rroot, in_sems.at[5]),
    ]
    for c in loads:
        c.start()
    load_b = pltpu.make_async_copy(inv_root.at[mine], blocks.at[mine_root, mine], in_sems.at[6])
    pl.when(x >= y)(load_b.start)

    barrier = pltpu.get_barrier_semaphore()
    for k in range(1, 16):
        pl.semaphore_signal(barrier, inc=1, device_id=ppart(k), device_id_type=MESH)
        pl.semaphore_signal(barrier, inc=1, device_id=gpart(k), device_id_type=MESH)

    load_r.wait()
    load_i.wait()

    for l in range(NL):
        fl[l * N:(l + 1) * N, :] = dot(il[l], rl[l]).astype(BF16)

    a1 = []
    for jj in range(4):
        b = lax.rem(y + jj, 4)
        load_c[jj].wait()
        for t in range(3):
            blk = pl.ds(pl.multiple_of(b * GB + t * 128, 128), 128)
            for l in range(NL):
                keep = pattern[l, b * 3 + t].astype(F32).astype(BF16)
                cl[l, blk, :] = cl[l, blk, :] * keep
        rb = rows(b, GB)
        acc = dot(jnp.concatenate([cl[l, rb, :] for l in range(NL)], axis=1), fl[...])
        if jj == 0:
            own1[...] = acc
        snd1[rows(jj, GB), :] = acc.astype(BF16)
        if jj == 1:
            pl.semaphore_wait(barrier, 30)
        for sent in {0: (), 1: (0, 1), 2: (2,), 3: (3,)}[jj]:
            for dx in range(4):
                k = dx * 4 + sent
                if k == 0:
                    continue
                piece = pl.ds(pl.multiple_of(sent * GB + lax.rem(x + dx, 4) * GP, 32), GP)
                a1.append(remote(snd1.at[piece], rcv1.at[k], s1.at[k], r1.at[k], ppart(k)))
                start(a1[-1:])

    pl.when(x >= y)(load_b.wait)
    rsend = [
        remote(blocks.at[mine_root, mine], blocks.at[mine_root, mine], sR.at[k], rR.at[k], ppart(k))
        for k in range(1, 16)
    ]
    start(rsend, x >= y)

    def leaf_transpose(l, carry):
        ct[l] = cl[l].T
        return carry

    lax.fori_loop(0, 2, leaf_transpose, 0)
    for c in loads:
        c.wait()
    gridT[...] = lg[...].T
    rootT_rhs[...] = rroot[...].astype(F32).T
    for k in range(1, 16):
        arrived([rsend[k - 1]], lax.rem(x - k // 4 + 4, 4) >= lax.rem(y - k % 4 + 4, 4))
    zsend = [
        remote(blocks.at[:, mine], blocks.at[:, mine], sC.at[k], rC.at[k], gpart(k)) for k in range(2, 16, 2)
    ]
    zpass = [remote(blocks.at[:, mine], blocks.at[:, mine], sC.at[1], rC.at[1], sibling)]
    start(zsend)
    start(zpass)
    my_piece = rows(x, GP)
    arrived(a1)
    tot = own1[my_piece, :]
    for k in range(1, 16):
        tot = tot + rcv1[k].astype(F32)
    rg[my_piece, :] = (rgrid[my_piece, :].astype(F32) - tot).astype(BF16)

    a2 = [remote(rg.at[my_piece], rg.at[my_piece], s2.at[k], r2.at[k], xpart(k)) for k in range(1, 4)]
    start(a2)
    lax.fori_loop(2, 4, leaf_transpose, 0)
    arrived(a2)
    partial = dot(lg[...], rg[...])
    part[...] = partial
    psnd[...] = partial.astype(BF16)
    a3 = [
        remote(psnd.at[rows(lax.rem(y + k, 4), GP)], rcv3.at[k], s3.at[k], r3.at[k], ypart(k))
        for k in range(1, 4)
    ]
    start(a3)
    lax.fori_loop(4, 6, leaf_transpose, 0)
    my_rows = rows(y, GP)
    arrived(a3)
    total = part[my_rows, :]
    for k in range(1, 4):
        total = total + rcv3[k].astype(F32)
    fg[my_rows, :] = total.astype(BF16)
    a3b = [remote(fg.at[my_rows], fg.at[my_rows], s3b.at[k], r3b.at[k], ypart(k)) for k in range(1, 4)]
    start(a3b)
    gsend = [remote(couple_grid.at[0], cg.at[y], sG.at[k], rG.at[k], ypart(k)) for k in range(1, 4)]

    for k in range(1, 4):
        start([gsend[k - 1]], lax.rem(y + k, 4) <= x)
    lax.fori_loop(6, 8, leaf_transpose, 0)
    arrived(a3b)
    up = dot(cg[y], fg[...]).T
    ut[...] = up
    usnd[...] = up.astype(BF16)
    a4 = [
        remote(usnd.at[rows(lax.rem(gz + k, 16), SLICE)], rcv4.at[k], s4.at[k], r4.at[k], gpart(k))
        for k in range(1, 16)
    ]
    start(a4)
    partial = dot(gridT[...], fg[...])
    hpart[...] = partial
    hsnd[...] = partial.astype(BF16)
    a8 = [
        remote(hsnd.at[rows(lax.rem(x + k, 4), GP)], rcv8.at[k], s8.at[k], r8.at[k], xpart(k))
        for k in range(1, 4)
    ]
    start(a8)
    for i, k in enumerate(range(2, 16, 2)):
        arrived([zsend[i]])
        from_z = rows(lax.rem(gz - k + 16, 16), SLICE)
        zpass.append(remote(blocks.at[:, from_z], blocks.at[:, from_z], sC.at[k + 1], rC.at[k + 1], sibling))
        start(zpass[-1:])
    arrived(a4)
    v = ut[mine, :]
    for k in range(1, 16):
        v = v + rcv4[k].astype(F32)
    w = (jnp.where(x == 0, rootT_rhs[mine, :], 0.0) - v).astype(BF16)
    wsnd[...] = w
    rcv5[here] = w
    a5 = [remote(wsnd, rcv5.at[here], s5.at[k], r5.at[k], ppart(k)) for k in range(1, 16)]
    start(a5)
    arrived(gsend, y <= x)

    @pl.when(y <= x)
    def _():
        for a in range(4):
            bsnd[a] = dot(cg[a], lg[...]).astype(BF16)

    bsend = [
        remote(bsnd.at[lax.rem(x + k, 4)], rcvb.at[k], sB.at[k], rB.at[k], xpart(k)) for k in range(1, 4)
    ]
    start(bsend, y <= x)
    arrived(a8)
    hpart[my_piece, :] += rcv8[1].astype(F32) + rcv8[2].astype(F32) + rcv8[3].astype(F32)
    arrived(zpass)
    arrived(a5)
    res = []
    for j in range(4):
        t = rcv5[j].astype(F32)
        for i in range(1, 4):
            t = t + rcv5[i * 4 + j].astype(F32)
        res.append(t.astype(BF16))
    zs = []
    for i in range(4):
        t = dot_nt(res[0], blocks[i * (i + 1) // 2])
        for j in range(1, i + 1):
            t = t + dot_nt(res[j], blocks[i * (i + 1) // 2 + j])
        zs.append(t.astype(BF16))
    for j in range(4):
        t = dot(zs[j], blocks[j * (j + 1) // 2 + j])
        for i in range(j + 1, 4):
            t = t + dot(zs[i], blocks[i * (i + 1) // 2 + j])
        rt[mine, j * RB:(j + 1) * RB] = t.astype(BF16)

    a6 = [remote(rt.at[mine], rt.at[mine], s6.at[k], r6.at[k], gpart(k)) for k in range(2, 16, 2)]
    start(a6)
    a6b = [remote(rt.at[mine], rt.at[mine], s6.at[1], r6.at[1], sibling)]
    start(a6b)
    bacc[...] = jnp.zeros_like(bacc)

    @pl.when(y <= x)
    def _():
        bacc[...] = bsnd[x].astype(F32)

    for k in range(1, 4):
        sent = lax.rem(x - k + 4, 4) >= y
        arrived([bsend[k - 1]], sent)

        @pl.when(sent)
        def _():
            bacc[...] += rcvb[k].astype(F32)

    bm[...] = bacc[...].astype(BF16)
    btm[...] = bm[...].T
    bts[x] = btm[my_piece, :]
    at = [
        remote(btm.at[rows(lax.rem(x + k, 4), GP)], bts.at[x], sT.at[k], rT.at[k], xpart(k))
        for k in range(1, 4)
    ]
    start(at)
    for i, k in enumerate(range(2, 16, 2)):
        arrived([a6[i]])
        from_z = rows(lax.rem(gz - k + 16, 16), SLICE)
        a6b.append(
            remote(rt.at[from_z], rt.at[from_z], s6.at[k + 1], r6.at[k + 1], sibling)
        )
        start(a6b[-1:])
    arrived(at)
    arrived(a6b)
    h = hpart[my_piece, :]
    for i in range(4):
        h = h - dot_nt(bts[i], rt[:, i * RB:(i + 1) * RB])
    home = rows(y * 4 + x, GP)
    xg[home, :] = h.astype(BF16)
    a9 = [remote(xg.at[home], xg.at[home], s9.at[k], r9.at[k], ppart(k)) for k in range(1, 16)]
    start([a9[k - 1] for k in (4, 8, 12, 1, 3, 5, 7, 9, 11, 13, 15, 2, 6, 10, 14)])
    stores = [pltpu.make_async_copy(rt.at[:, rows(y, RB)], out_root, out_sems.at[2])]
    stores[0].start()
    odd = lax.rem(y, 2) == 1
    for k in range(1, 16):
        dy = k % 4
        if dy == 0:
            arrived(a9[k - 1:k])
        elif dy == 1:
            arrived(a9[k - 1:k], odd)
        elif dy == 3:
            arrived(a9[k - 1:k], jnp.logical_not(odd))
    top = pl.ds(pl.multiple_of((y // 2) * HALF, HALF), HALF)
    for g in range(2):
        ls = slice(g * 4, g * 4 + 4)
        t = dot(ct[ls, :, top].reshape(4 * N, HALF), xg[top, :])
        gs = slice(g * 4 * N, (g + 1) * 4 * N)
        ol[gs, :] = fl[gs, :].astype(F32) - t
    for k in range(1, 16):
        dy = k % 4
        if dy == 2:
            arrived(a9[k - 1:k])
        elif dy == 1:
            arrived(a9[k - 1:k], jnp.logical_not(odd))
        elif dy == 3:
            arrived(a9[k - 1:k], odd)
    rest = pl.ds(pl.multiple_of((1 - y // 2) * HALF, HALF), HALF)
    for g in range(2):
        gs = slice(g * 4 * N, (g + 1) * 4 * N)
        t = dot(ct[g * 4:g * 4 + 4, :, rest].reshape(4 * N, HALF), xg[rest, :])
        back[gs, :] = (ol[gs, :] - t).astype(BF16)
        stores.append(pltpu.make_async_copy(back.at[gs], out_back.at[gs], out_sems.at[g]))
        stores[-1].start()
    stores.append(pltpu.make_async_copy(xg.at[rows(y, GB)], out_top, out_sems.at[3]))
    stores[-1].start()
    finish()
    for c in stores:
        c.wait()


def leaves_back(
    inv_leaf, res_leaf, top, root, out_leaf, out_grid, out_root,
    il, bk, tp, rt, sol, og, oroot, i_sems, b_sems, sems,
):
    loads = []
    for l in range(NL):
        loads.append((
            pltpu.make_async_copy(inv_leaf.at[l], il.at[l], i_sems.at[l]),
            pltpu.make_async_copy(res_leaf.at[pl.ds(l * N, N)], bk.at[l], b_sems.at[l]),
        ))
        for c in loads[l]:
            c.start()
    small = [pltpu.make_async_copy(top, tp, sems.at[NL + 2]), pltpu.make_async_copy(root, rt, sems.at[NL + 3])]
    for c in small:
        c.start()
    copies = []
    for l in range(NL):
        for c in loads[l]:
            c.wait()
        sol[l] = dot_tn(il[l], bk[l])
        copies.append(pltpu.make_async_copy(sol.at[l], out_leaf.at[l], sems.at[l]))
        copies[-1].start()
    for c in small:
        c.wait()
    og[...] = tp[...].astype(F32)
    copies.append(pltpu.make_async_copy(og, out_grid.at[0], sems.at[NL]))
    copies[-1].start()
    oroot[...] = rt[...].astype(F32).T
    copies.append(pltpu.make_async_copy(oroot, out_root, sems.at[NL + 1]))
    copies[-1].start()
    for c in copies:
        c.wait()


def on_device(*args):
    vm = pltpu.VMEM
    dma = pltpu.SemaphoreType.DMA
    hbm = pl.BlockSpec(memory_space=pl.ANY)
    smem = pl.BlockSpec(memory_space=pltpu.SMEM)
    kept = pl.pallas_call(
        kernel,
        out_shape=(
            jax.ShapeDtypeStruct((NL * N, NRHS), BF16),
            jax.ShapeDtypeStruct((GB, NRHS), BF16),
            jax.ShapeDtypeStruct((NRHS, RB), BF16),
        ),
        in_specs=[hbm, hbm, hbm, smem, hbm, hbm, hbm, hbm, hbm],
        out_specs=(hbm, hbm, hbm),
        scratch_shapes=[
            vm((NL, N, NRHS), BF16), vm((NL, N, N), BF16), vm((NL, SG, N), BF16),
            vm((NL * N, NRHS), BF16), vm((NL, N, SG), BF16), vm((NL * N, NRHS), F32),
            vm((NL * N, NRHS), BF16), vm((SG, NRHS), BF16), vm((GB, GB), BF16), vm((GB, NRHS), BF16), vm((RB, NRHS), BF16),
            vm((4, RB, GB), BF16), vm((4, RB, GB), BF16), vm((4, RB, GB), BF16), vm((RB, GB), F32),
            vm((RB, GB), BF16), vm((GB, RB), BF16), vm((4, GP, RB), BF16),
            vm((GB, NRHS), F32), vm((SG, NRHS), BF16), vm((16, GP, NRHS), BF16),
            vm((GB, NRHS), BF16), vm((GB, NRHS), F32), vm((GB, NRHS), BF16),
            vm((4, GP, NRHS), BF16), vm((GB, NRHS), BF16), vm((GB, GB), BF16),
            vm((GB, NRHS), F32), vm((GB, NRHS), BF16), vm((4, GP, NRHS), BF16),
            vm((NRHS, RB), F32), vm((NRHS, RB), BF16), vm((16, SLICE, RB), BF16),
            vm((NRHS, RB), F32), vm((16, SLICE, RB), BF16), vm((SLICE, RB), BF16),
            vm((10, RB, RB), BF16), vm((NRHS, 4 * RB), BF16),
            dma((7,)), dma((4,)), dma((4,)),
            dma((16,)), dma((16,)), dma((4,)), dma((4,)), dma((4,)), dma((4,)), dma((4,)), dma((4,)),
            dma((16,)), dma((16,)), dma((16,)), dma((16,)), dma((16,)), dma((16,)),
            dma((4,)), dma((4,)), dma((16,)), dma((16,)),
            dma((16,)), dma((16,)), dma((16,)), dma((16,)), dma((4,)), dma((4,)), dma((4,)), dma((4,)),
            dma((4,)), dma((4,)),
        ],
        compiler_params=pltpu.CompilerParams(
            collective_id=0, has_side_effects=True, vmem_limit_bytes=62 << 20
        ),
        cost_estimate=pl.CostEstimate(flops=4_200_000_000, bytes_accessed=13_000_000, transcendentals=0),
        name="solve",
    )(*args)
    return pl.pallas_call(
        leaves_back,
        out_shape=(
            jax.ShapeDtypeStruct((NL, N, NRHS), F32),
            jax.ShapeDtypeStruct((1, GB, NRHS), F32),
            jax.ShapeDtypeStruct((RB, NRHS), F32),
        ),
        in_specs=[hbm] * 4,
        out_specs=(hbm, hbm, hbm),
        scratch_shapes=[
            vm((NL, N, N), BF16), vm((NL, N, NRHS), BF16), vm((GB, NRHS), BF16), vm((NRHS, RB), BF16),
            vm((NL, N, NRHS), F32), vm((GB, NRHS), F32), vm((RB, NRHS), F32),
            dma((NL,)), dma((NL,)), dma((NL + 4,)),
        ],
        compiler_params=pltpu.CompilerParams(vmem_limit_bytes=62 << 20),
        cost_estimate=pl.CostEstimate(flops=270_000_000, bytes_accessed=4_800_000, transcendentals=0),
        name="leaves_back",
    )(args[1], *kept)


def solution(mesh):
    return jax.shard_map(
        on_device,
        mesh=mesh,
        in_specs=(
            P(("gz", "row", "col"), None, None),
            P(("gz", "row", "col"), None, None),
            P(("gz", "row", "col"), None, None),
            P(("gz", "row", "col"), None),
            P("gz", "col", None),
            P("gz", "row", "col"),
            P("gz", "col", "row"),
            P("col", None),
            P("row", "col"),
        ),
        out_specs=(P(("gz", "row", "col"), None, None), P("gz", "col", None), P("col", None)),
        check_vma=False,
    )
```

```python
import jax
import jax.numpy as jnp
from jax import lax
from jax.experimental import pallas as pl
from jax.experimental.pallas import tpu as pltpu
from jax.sharding import PartitionSpec as P

MESH = pl.DeviceIdType.MESH
F32 = jnp.float32
BF16 = jnp.bfloat16

NL = 8
N = 256
GB = 384
GP = 96
SG = 1536
RB = 256
NRHS = 256
HALF = SG // 2
SLICE = 16


def dot(a, b):
    return jnp.dot(a, b, preferred_element_type=F32)


def dot_nt(a, b):
    return lax.dot_general(a, b, (((1,), (1,)), ((), ())), preferred_element_type=F32)


def dot_tn(a, b):
    return lax.dot_general(a, b, (((0,), (0,)), ((), ())), preferred_element_type=F32)


def kernel(
    rhs_leaf, inv_leaf, couple_leaf, pattern, rhs_grid, inv_grid, couple_grid, rhs_root, inv_root,
    out_back, out_top, out_root,
    rl, il, cl, fl, ct, ol, back, xg, lg, rgrid, rroot,
    cg, bsnd, rcvb, bacc, bm, btm, bts,
    own1, snd1, rcv1, rg, part, psnd, rcv3, fg, gridT, hpart, hsnd, rcv8,
    ut, usnd, rcv4, rootT_rhs, rcv5, wsnd, blocks, rt,
    in_sems, c_sems, out_sems,
    s1, r1, s2, r2, s3, r3, s3b, r3b, s4, r4, s5, r5, s6, r6, s8, r8, s9, r9,
    sR, rR, sC, rC, sG, rG, sB, rB, sT, rT,
):
    gz = lax.axis_index("gz")
    x = lax.axis_index("row")
    y = lax.axis_index("col")
    core = lax.rem(gz, 2)
    sibling = (gz + 1 - 2 * core, x, y)
    here = x * 4 + y

    def xpart(k):
        return (gz, lax.rem(x + k, 4), y)

    def ypart(k):
        return (gz, x, lax.rem(y + k, 4))

    def gpart(k):
        return (lax.rem(gz + k, 16), x, y)

    def ppart(k):
        return (gz, lax.rem(x + k // 4, 4), lax.rem(y + k % 4, 4))

    def remote(src, dst, ssem, rsem, dev):
        return pltpu.make_async_remote_copy(
            src_ref=src, dst_ref=dst, send_sem=ssem, recv_sem=rsem, device_id=dev, device_id_type=MESH
        )

    def rows(i, n):
        return pl.ds(pl.multiple_of(i * n, n), n)

    pending = []

    def start(copies, when=None):
        for c in copies:
            if when is None:
                c.start()
            else:
                pl.when(when)(c.start)
            pending.append((c, when))

    def arrived(copies, when=None):
        for c in copies:
            if when is None:
                c.wait_recv()
            else:
                pl.when(when)(c.wait_recv)

    def finish():
        for c, when in pending:
            if when is None:
                c.wait_send()
            else:
                pl.when(when)(c.wait_send)

    mine = rows(gz, SLICE)
    mine_root = x * (x + 1) // 2 + y
    load_r = pltpu.make_async_copy(rhs_leaf, rl, in_sems.at[0])
    load_i = pltpu.make_async_copy(inv_leaf, il, in_sems.at[1])
    load_r.start()
    load_i.start()
    load_c = []
    for jj in range(4):
        block = rows(lax.rem(y + jj, 4), GB)
        load_c.append(pltpu.make_async_copy(couple_leaf.at[:, block], cl.at[:, block], c_sems.at[jj]))
        load_c[-1].start()
    loads = [
        pltpu.make_async_copy(couple_grid.at[0], cg.at[y], in_sems.at[2]),
        pltpu.make_async_copy(inv_grid.at[0], lg, in_sems.at[3]),
        pltpu.make_async_copy(rhs_grid.at[0], rgrid, in_sems.at[4]),
        pltpu.make_async_copy(rhs_root, rroot, in_sems.at[5]),
    ]
    for c in loads:
        c.start()
    load_b = pltpu.make_async_copy(inv_root.at[mine], blocks.at[mine_root, mine], in_sems.at[6])
    pl.when(x >= y)(load_b.start)

    barrier = pltpu.get_barrier_semaphore()
    for k in range(1, 16):
        pl.semaphore_signal(barrier, inc=1, device_id=ppart(k), device_id_type=MESH)
        pl.semaphore_signal(barrier, inc=1, device_id=gpart(k), device_id_type=MESH)

    load_r.wait()
    load_i.wait()

    for l in range(NL):
        fl[l * N:(l + 1) * N, :] = dot(il[l], rl[l]).astype(BF16)

    a1 = []
    for jj in range(4):
        b = lax.rem(y + jj, 4)
        load_c[jj].wait()
        for t in range(3):
            blk = pl.ds(pl.multiple_of(b * GB + t * 128, 128), 128)
            for l in range(NL):
                keep = pattern[l, b * 3 + t].astype(F32).astype(BF16)
                cl[l, blk, :] = cl[l, blk, :] * keep
        rb = rows(b, GB)
        acc = dot(jnp.concatenate([cl[l, rb, :] for l in range(NL)], axis=1), fl[...])
        if jj == 0:
            own1[...] = acc
        snd1[rows(jj, GB), :] = acc.astype(BF16)
        if jj == 1:
            pl.semaphore_wait(barrier, 30)
        for sent in {0: (), 1: (0, 1), 2: (2,), 3: (3,)}[jj]:
            for dx in range(4):
                k = dx * 4 + sent
                if k == 0:
                    continue
                piece = pl.ds(pl.multiple_of(sent * GB + lax.rem(x + dx, 4) * GP, 32), GP)
                a1.append(remote(snd1.at[piece], rcv1.at[k], s1.at[k], r1.at[k], ppart(k)))
                start(a1[-1:])

    pl.when(x >= y)(load_b.wait)
    rsend = [
        remote(blocks.at[mine_root, mine], blocks.at[mine_root, mine], sR.at[k], rR.at[k], ppart(k))
        for k in range(1, 16)
    ]
    start(rsend, x >= y)

    def leaf_transpose(l, carry):
        ct[l] = cl[l].T
        return carry

    lax.fori_loop(0, 2, leaf_transpose, 0)
    for c in loads:
        c.wait()
    gridT[...] = lg[...].T
    rootT_rhs[...] = rroot[...].astype(F32).T
    for k in range(1, 16):
        arrived([rsend[k - 1]], lax.rem(x - k // 4 + 4, 4) >= lax.rem(y - k % 4 + 4, 4))
    zsend = [
        remote(blocks.at[:, mine], blocks.at[:, mine], sC.at[k], rC.at[k], gpart(k)) for k in range(2, 16, 2)
    ]
    zpass = [remote(blocks.at[:, mine], blocks.at[:, mine], sC.at[1], rC.at[1], sibling)]
    start(zsend)
    start(zpass)
    my_piece = rows(x, GP)
    arrived(a1)
    tot = own1[my_piece, :]
    for k in range(1, 16):
        tot = tot + rcv1[k].astype(F32)
    rg[my_piece, :] = (rgrid[my_piece, :].astype(F32) - tot).astype(BF16)

    a2 = [remote(rg.at[my_piece], rg.at[my_piece], s2.at[k], r2.at[k], xpart(k)) for k in range(1, 4)]
    start(a2)
    lax.fori_loop(2, 4, leaf_transpose, 0)
    arrived(a2)
    partial = dot(lg[...], rg[...])
    part[...] = partial
    psnd[...] = partial.astype(BF16)
    a3 = [
        remote(psnd.at[rows(lax.rem(y + k, 4), GP)], rcv3.at[k], s3.at[k], r3.at[k], ypart(k))
        for k in range(1, 4)
    ]
    start(a3)
    lax.fori_loop(4, 6, leaf_transpose, 0)
    my_rows = rows(y, GP)
    arrived(a3)
    total = part[my_rows, :]
    for k in range(1, 4):
        total = total + rcv3[k].astype(F32)
    fg[my_rows, :] = total.astype(BF16)
    a3b = [remote(fg.at[my_rows], fg.at[my_rows], s3b.at[k], r3b.at[k], ypart(k)) for k in range(1, 4)]
    start(a3b)
    gsend = [remote(couple_grid.at[0], cg.at[y], sG.at[k], rG.at[k], ypart(k)) for k in range(1, 4)]

    for k in range(1, 4):
        start([gsend[k - 1]], lax.rem(y + k, 4) <= x)
    lax.fori_loop(6, 8, leaf_transpose, 0)
    arrived(a3b)
    up = dot(cg[y], fg[...]).T
    ut[...] = up
    usnd[...] = up.astype(BF16)
    a4 = [
        remote(usnd.at[rows(lax.rem(gz + k, 16), SLICE)], rcv4.at[k], s4.at[k], r4.at[k], gpart(k))
        for k in range(1, 16)
    ]
    start(a4)
    partial = dot(gridT[...], fg[...])
    hpart[...] = partial
    hsnd[...] = partial.astype(BF16)
    a8 = [
        remote(hsnd.at[rows(lax.rem(x + k, 4), GP)], rcv8.at[k], s8.at[k], r8.at[k], xpart(k))
        for k in range(1, 4)
    ]
    start(a8)
    for i, k in enumerate(range(2, 16, 2)):
        arrived([zsend[i]])
        from_z = rows(lax.rem(gz - k + 16, 16), SLICE)
        zpass.append(remote(blocks.at[:, from_z], blocks.at[:, from_z], sC.at[k + 1], rC.at[k + 1], sibling))
        start(zpass[-1:])
    arrived(a4)
    v = ut[mine, :]
    for k in range(1, 16):
        v = v + rcv4[k].astype(F32)
    w = (jnp.where(x == 0, rootT_rhs[mine, :], 0.0) - v).astype(BF16)
    wsnd[...] = w
    rcv5[here] = w
    a5 = [remote(wsnd, rcv5.at[here], s5.at[k], r5.at[k], ppart(k)) for k in range(1, 16)]
    start(a5)
    arrived(gsend, y <= x)

    @pl.when(y <= x)
    def _():
        for a in range(4):
            bsnd[a] = dot(cg[a], lg[...]).astype(BF16)

    bsend = [
        remote(bsnd.at[lax.rem(x + k, 4)], rcvb.at[k], sB.at[k], rB.at[k], xpart(k)) for k in range(1, 4)
    ]
    start(bsend, y <= x)
    arrived(a8)
    hpart[my_piece, :] += rcv8[1].astype(F32) + rcv8[2].astype(F32) + rcv8[3].astype(F32)
    arrived(zpass)
    arrived(a5)
    res = []
    for j in range(4):
        t = rcv5[j].astype(F32)
        for i in range(1, 4):
            t = t + rcv5[i * 4 + j].astype(F32)
        res.append(t.astype(BF16))
    zs = []
    for i in range(4):
        t = dot_nt(res[0], blocks[i * (i + 1) // 2])
        for j in range(1, i + 1):
            t = t + dot_nt(res[j], blocks[i * (i + 1) // 2 + j])
        zs.append(t.astype(BF16))
    for j in range(4):
        t = dot(zs[j], blocks[j * (j + 1) // 2 + j])
        for i in range(j + 1, 4):
            t = t + dot(zs[i], blocks[i * (i + 1) // 2 + j])
        rt[mine, j * RB:(j + 1) * RB] = t.astype(BF16)

    a6 = [remote(rt.at[mine], rt.at[mine], s6.at[k], r6.at[k], gpart(k)) for k in range(2, 16, 2)]
    start(a6)
    a6b = [remote(rt.at[mine], rt.at[mine], s6.at[1], r6.at[1], sibling)]
    start(a6b)
    bacc[...] = jnp.zeros_like(bacc)

    @pl.when(y <= x)
    def _():
        bacc[...] = bsnd[x].astype(F32)

    for k in range(1, 4):
        sent = lax.rem(x - k + 4, 4) >= y
        arrived([bsend[k - 1]], sent)

        @pl.when(sent)
        def _():
            bacc[...] += rcvb[k].astype(F32)

    bm[...] = bacc[...].astype(BF16)
    btm[...] = bm[...].T
    bts[x] = btm[my_piece, :]
    at = [
        remote(btm.at[rows(lax.rem(x + k, 4), GP)], bts.at[x], sT.at[k], rT.at[k], xpart(k))
        for k in range(1, 4)
    ]
    start(at)
    for i, k in enumerate(range(2, 16, 2)):
        arrived([a6[i]])
        from_z = rows(lax.rem(gz - k + 16, 16), SLICE)
        a6b.append(
            remote(rt.at[from_z], rt.at[from_z], s6.at[k + 1], r6.at[k + 1], sibling)
        )
        start(a6b[-1:])
    arrived(at)
    arrived(a6b)
    h = hpart[my_piece, :]
    for i in range(4):
        h = h - dot_nt(bts[i], rt[:, i * RB:(i + 1) * RB])
    home = rows(y * 4 + x, GP)
    xg[home, :] = h.astype(BF16)
    a9 = [remote(xg.at[home], xg.at[home], s9.at[k], r9.at[k], ppart(k)) for k in range(1, 16)]
    start([a9[k - 1] for k in (4, 8, 12, 1, 3, 5, 7, 9, 11, 13, 15, 2, 6, 10, 14)])
    stores = [pltpu.make_async_copy(rt.at[:, rows(y, RB)], out_root, out_sems.at[2])]
    stores[0].start()
    odd = lax.rem(y, 2) == 1
    for k in range(1, 16):
        dy = k % 4
        if dy == 0:
            arrived(a9[k - 1:k])
        elif dy == 1:
            arrived(a9[k - 1:k], odd)
        elif dy == 3:
            arrived(a9[k - 1:k], jnp.logical_not(odd))
    top = pl.ds(pl.multiple_of((y // 2) * HALF, HALF), HALF)
    for g in range(2):
        ls = slice(g * 4, g * 4 + 4)
        t = dot(ct[ls, :, top].reshape(4 * N, HALF), xg[top, :])
        gs = slice(g * 4 * N, (g + 1) * 4 * N)
        ol[gs, :] = fl[gs, :].astype(F32) - t
    for k in range(1, 16):
        dy = k % 4
        if dy == 2:
            arrived(a9[k - 1:k])
        elif dy == 1:
            arrived(a9[k - 1:k], jnp.logical_not(odd))
        elif dy == 3:
            arrived(a9[k - 1:k], odd)
    stores.append(pltpu.make_async_copy(xg.at[rows(y, GB)], out_top, out_sems.at[3]))
    stores[-1].start()
    rest = pl.ds(pl.multiple_of((1 - y // 2) * HALF, HALF), HALF)
    for g in range(2):
        gs = slice(g * 4 * N, (g + 1) * 4 * N)
        t = dot(ct[g * 4:g * 4 + 4, :, rest].reshape(4 * N, HALF), xg[rest, :])
        back[gs, :] = (ol[gs, :] - t).astype(BF16)
        stores.append(pltpu.make_async_copy(back.at[gs], out_back.at[gs], out_sems.at[g]))
        stores[-1].start()
    finish()
    for c in stores:
        c.wait()


def leaves_back(
    inv_leaf, res_leaf, top, root, out_leaf, out_grid, out_root,
    il, bk, tp, rt, sol, og, oroot, i_sems, b_sems, sems,
):
    loads = []
    for l in range(NL):
        loads.append((
            pltpu.make_async_copy(inv_leaf.at[l], il.at[l], i_sems.at[l]),
            pltpu.make_async_copy(res_leaf.at[pl.ds(l * N, N)], bk.at[l], b_sems.at[l]),
        ))
        for c in loads[l]:
            c.start()
    small = [pltpu.make_async_copy(top, tp, sems.at[NL + 2]), pltpu.make_async_copy(root, rt, sems.at[NL + 3])]
    for c in small:
        c.start()
    copies = []
    for l in range(NL):
        for c in loads[l]:
            c.wait()
        sol[l] = dot_tn(il[l], bk[l])
        copies.append(pltpu.make_async_copy(sol.at[l], out_leaf.at[l], sems.at[l]))
        copies[-1].start()
        if l == 3:
            for c in small:
                c.wait()
            og[...] = tp[...].astype(F32)
            copies.append(pltpu.make_async_copy(og, out_grid.at[0], sems.at[NL]))
            copies[-1].start()
            oroot[...] = rt[...].astype(F32).T
            copies.append(pltpu.make_async_copy(oroot, out_root, sems.at[NL + 1]))
            copies[-1].start()
    for c in copies:
        c.wait()


def on_device(*args):
    vm = pltpu.VMEM
    dma = pltpu.SemaphoreType.DMA
    hbm = pl.BlockSpec(memory_space=pl.ANY)
    smem = pl.BlockSpec(memory_space=pltpu.SMEM)
    kept = pl.pallas_call(
        kernel,
        out_shape=(
            jax.ShapeDtypeStruct((NL * N, NRHS), BF16),
            jax.ShapeDtypeStruct((GB, NRHS), BF16),
            jax.ShapeDtypeStruct((NRHS, RB), BF16),
        ),
        in_specs=[hbm, hbm, hbm, smem, hbm, hbm, hbm, hbm, hbm],
        out_specs=(hbm, hbm, hbm),
        scratch_shapes=[
            vm((NL, N, NRHS), BF16), vm((NL, N, N), BF16), vm((NL, SG, N), BF16),
            vm((NL * N, NRHS), BF16), vm((NL, N, SG), BF16), vm((NL * N, NRHS), F32),
            vm((NL * N, NRHS), BF16), vm((SG, NRHS), BF16), vm((GB, GB), BF16), vm((GB, NRHS), BF16), vm((RB, NRHS), BF16),
            vm((4, RB, GB), BF16), vm((4, RB, GB), BF16), vm((4, RB, GB), BF16), vm((RB, GB), F32),
            vm((RB, GB), BF16), vm((GB, RB), BF16), vm((4, GP, RB), BF16),
            vm((GB, NRHS), F32), vm((SG, NRHS), BF16), vm((16, GP, NRHS), BF16),
            vm((GB, NRHS), BF16), vm((GB, NRHS), F32), vm((GB, NRHS), BF16),
            vm((4, GP, NRHS), BF16), vm((GB, NRHS), BF16), vm((GB, GB), BF16),
            vm((GB, NRHS), F32), vm((GB, NRHS), BF16), vm((4, GP, NRHS), BF16),
            vm((NRHS, RB), F32), vm((NRHS, RB), BF16), vm((16, SLICE, RB), BF16),
            vm((NRHS, RB), F32), vm((16, SLICE, RB), BF16), vm((SLICE, RB), BF16),
            vm((10, RB, RB), BF16), vm((NRHS, 4 * RB), BF16),
            dma((7,)), dma((4,)), dma((4,)),
            dma((16,)), dma((16,)), dma((4,)), dma((4,)), dma((4,)), dma((4,)), dma((4,)), dma((4,)),
            dma((16,)), dma((16,)), dma((16,)), dma((16,)), dma((16,)), dma((16,)),
            dma((4,)), dma((4,)), dma((16,)), dma((16,)),
            dma((16,)), dma((16,)), dma((16,)), dma((16,)), dma((4,)), dma((4,)), dma((4,)), dma((4,)),
            dma((4,)), dma((4,)),
        ],
        compiler_params=pltpu.CompilerParams(
            collective_id=0, has_side_effects=True, vmem_limit_bytes=62 << 20
        ),
        cost_estimate=pl.CostEstimate(flops=4_200_000_000, bytes_accessed=13_000_000, transcendentals=0),
        name="solve",
    )(*args)
    return pl.pallas_call(
        leaves_back,
        out_shape=(
            jax.ShapeDtypeStruct((NL, N, NRHS), F32),
            jax.ShapeDtypeStruct((1, GB, NRHS), F32),
            jax.ShapeDtypeStruct((RB, NRHS), F32),
        ),
        in_specs=[hbm] * 4,
        out_specs=(hbm, hbm, hbm),
        scratch_shapes=[
            vm((NL, N, N), BF16), vm((NL, N, NRHS), BF16), vm((GB, NRHS), BF16), vm((NRHS, RB), BF16),
            vm((NL, N, NRHS), F32), vm((GB, NRHS), F32), vm((RB, NRHS), F32),
            dma((NL,)), dma((NL,)), dma((NL + 4,)),
        ],
        compiler_params=pltpu.CompilerParams(vmem_limit_bytes=62 << 20),
        cost_estimate=pl.CostEstimate(flops=270_000_000, bytes_accessed=4_800_000, transcendentals=0),
        name="leaves_back",
    )(args[1], *kept)


def solution(mesh):
    return jax.shard_map(
        on_device,
        mesh=mesh,
        in_specs=(
            P(("gz", "row", "col"), None, None),
            P(("gz", "row", "col"), None, None),
            P(("gz", "row", "col"), None, None),
            P(("gz", "row", "col"), None),
            P("gz", "col", None),
            P("gz", "row", "col"),
            P("gz", "col", "row"),
            P("col", None),
            P("row", "col"),
        ),
        out_specs=(P(("gz", "row", "col"), None, None), P("gz", "col", None), P("col", None)),
        check_vma=False,
    )
```

```python
import jax
import jax.numpy as jnp
from jax import lax
from jax.experimental import pallas as pl
from jax.experimental.pallas import tpu as pltpu
from jax.sharding import PartitionSpec as P

MESH = pl.DeviceIdType.MESH
F32 = jnp.float32
BF16 = jnp.bfloat16

NL = 8
N = 256
GB = 384
GP = 96
SG = 1536
RB = 256
NRHS = 256
HALF = SG // 2
SLICE = 16


def dot(a, b):
    return jnp.dot(a, b, preferred_element_type=F32)


def dot_nt(a, b):
    return lax.dot_general(a, b, (((1,), (1,)), ((), ())), preferred_element_type=F32)


def dot_tn(a, b):
    return lax.dot_general(a, b, (((0,), (0,)), ((), ())), preferred_element_type=F32)


def kernel(
    rhs_leaf, inv_leaf, couple_leaf, pattern, rhs_grid, inv_grid, couple_grid, rhs_root, inv_root,
    out_back, out_top, out_root,
    rl, il, cl, fl, ct, ol, back, xg, lg, rgrid, rroot,
    cg, bsnd, rcvb, bacc, bm, btm, bts,
    own1, snd1, rcv1, rg, part, psnd, rcv3, fg, gridT, hpart, hsnd, rcv8,
    ut, usnd, rcv4, rootT_rhs, rcv5, wsnd, blocks, rt,
    in_sems, c_sems, out_sems,
    s1, r1, s2, r2, s3, r3, s3b, r3b, s4, r4, s5, r5, s6, r6, s8, r8, s9, r9,
    sR, rR, sC, rC, sG, rG, sB, rB, sT, rT,
):
    gz = lax.axis_index("gz")
    x = lax.axis_index("row")
    y = lax.axis_index("col")
    core = lax.rem(gz, 2)
    sibling = (gz + 1 - 2 * core, x, y)
    here = x * 4 + y

    def xpart(k):
        return (gz, lax.rem(x + k, 4), y)

    def ypart(k):
        return (gz, x, lax.rem(y + k, 4))

    def gpart(k):
        return (lax.rem(gz + k, 16), x, y)

    def ppart(k):
        return (gz, lax.rem(x + k // 4, 4), lax.rem(y + k % 4, 4))

    def remote(src, dst, ssem, rsem, dev):
        return pltpu.make_async_remote_copy(
            src_ref=src, dst_ref=dst, send_sem=ssem, recv_sem=rsem, device_id=dev, device_id_type=MESH
        )

    def rows(i, n):
        return pl.ds(pl.multiple_of(i * n, n), n)

    pending = []

    def start(copies, when=None):
        for c in copies:
            if when is None:
                c.start()
            else:
                pl.when(when)(c.start)
            pending.append((c, when))

    def arrived(copies, when=None):
        for c in copies:
            if when is None:
                c.wait_recv()
            else:
                pl.when(when)(c.wait_recv)

    def finish():
        for c, when in pending:
            if when is None:
                c.wait_send()
            else:
                pl.when(when)(c.wait_send)

    mine = rows(gz, SLICE)
    mine_root = x * (x + 1) // 2 + y
    load_r = pltpu.make_async_copy(rhs_leaf, rl, in_sems.at[0])
    load_i = pltpu.make_async_copy(inv_leaf, il, in_sems.at[1])
    load_r.start()
    load_i.start()
    load_c = []
    for jj in range(4):
        block = rows(lax.rem(y + jj, 4), GB)
        load_c.append(pltpu.make_async_copy(couple_leaf.at[:, block], cl.at[:, block], c_sems.at[jj]))
        load_c[-1].start()
    loads = [
        pltpu.make_async_copy(couple_grid.at[0], cg.at[y], in_sems.at[2]),
        pltpu.make_async_copy(inv_grid.at[0], lg, in_sems.at[3]),
        pltpu.make_async_copy(rhs_grid.at[0], rgrid, in_sems.at[4]),
        pltpu.make_async_copy(rhs_root, rroot, in_sems.at[5]),
    ]
    for c in loads:
        c.start()
    load_b = pltpu.make_async_copy(inv_root.at[mine], blocks.at[mine_root, mine], in_sems.at[6])
    pl.when(x >= y)(load_b.start)

    barrier = pltpu.get_barrier_semaphore()
    for k in range(1, 16):
        pl.semaphore_signal(barrier, inc=1, device_id=ppart(k), device_id_type=MESH)
        pl.semaphore_signal(barrier, inc=1, device_id=gpart(k), device_id_type=MESH)

    load_r.wait()
    load_i.wait()

    for l in range(NL):
        fl[l * N:(l + 1) * N, :] = dot(il[l], rl[l]).astype(BF16)

    a1 = []
    for jj in range(4):
        b = lax.rem(y + jj, 4)
        load_c[jj].wait()
        for t in range(3):
            blk = pl.ds(pl.multiple_of(b * GB + t * 128, 128), 128)
            for l in range(NL):
                keep = pattern[l, b * 3 + t].astype(F32).astype(BF16)
                cl[l, blk, :] = cl[l, blk, :] * keep
        rb = rows(b, GB)
        acc = dot(jnp.concatenate([cl[l, rb, :] for l in range(NL)], axis=1), fl[...])
        if jj == 0:
            own1[...] = acc
        snd1[rows(jj, GB), :] = acc.astype(BF16)
        if jj == 0:
            pl.semaphore_wait(barrier, 30)
        for sent in (jj,):
            for dx in range(4):
                k = dx * 4 + sent
                if k == 0:
                    continue
                piece = pl.ds(pl.multiple_of(sent * GB + lax.rem(x + dx, 4) * GP, 32), GP)
                a1.append(remote(snd1.at[piece], rcv1.at[k], s1.at[k], r1.at[k], ppart(k)))
                start(a1[-1:])

    pl.when(x >= y)(load_b.wait)
    rsend = [
        remote(blocks.at[mine_root, mine], blocks.at[mine_root, mine], sR.at[k], rR.at[k], ppart(k))
        for k in range(1, 16)
    ]
    start(rsend, x >= y)

    def leaf_transpose(l, carry):
        ct[l] = cl[l].T
        return carry

    lax.fori_loop(0, 2, leaf_transpose, 0)
    for c in loads:
        c.wait()
    gridT[...] = lg[...].T
    rootT_rhs[...] = rroot[...].astype(F32).T
    for k in range(1, 16):
        arrived([rsend[k - 1]], lax.rem(x - k // 4 + 4, 4) >= lax.rem(y - k % 4 + 4, 4))
    zsend = [
        remote(blocks.at[:, mine], blocks.at[:, mine], sC.at[k], rC.at[k], gpart(k)) for k in range(2, 16, 2)
    ]
    zpass = [remote(blocks.at[:, mine], blocks.at[:, mine], sC.at[1], rC.at[1], sibling)]
    start(zsend)
    start(zpass)
    my_piece = rows(x, GP)
    arrived(a1)
    tot = own1[my_piece, :]
    for k in range(1, 16):
        tot = tot + rcv1[k].astype(F32)
    rg[my_piece, :] = (rgrid[my_piece, :].astype(F32) - tot).astype(BF16)

    a2 = [remote(rg.at[my_piece], rg.at[my_piece], s2.at[k], r2.at[k], xpart(k)) for k in range(1, 4)]
    start(a2)
    lax.fori_loop(2, 4, leaf_transpose, 0)
    arrived(a2)
    partial = dot(lg[...], rg[...])
    part[...] = partial
    psnd[...] = partial.astype(BF16)
    a3 = [
        remote(psnd.at[rows(lax.rem(y + k, 4), GP)], rcv3.at[k], s3.at[k], r3.at[k], ypart(k))
        for k in range(1, 4)
    ]
    start(a3)
    lax.fori_loop(4, 6, leaf_transpose, 0)
    my_rows = rows(y, GP)
    arrived(a3)
    total = part[my_rows, :]
    for k in range(1, 4):
        total = total + rcv3[k].astype(F32)
    fg[my_rows, :] = total.astype(BF16)
    a3b = [remote(fg.at[my_rows], fg.at[my_rows], s3b.at[k], r3b.at[k], ypart(k)) for k in range(1, 4)]
    start(a3b)
    gsend = [remote(couple_grid.at[0], cg.at[y], sG.at[k], rG.at[k], ypart(k)) for k in range(1, 4)]

    for k in range(1, 4):
        start([gsend[k - 1]], lax.rem(y + k, 4) <= x)
    lax.fori_loop(6, 8, leaf_transpose, 0)
    arrived(a3b)
    up = dot(cg[y], fg[...]).T
    ut[...] = up
    usnd[...] = up.astype(BF16)
    a4 = [
        remote(usnd.at[rows(lax.rem(gz + k, 16), SLICE)], rcv4.at[k], s4.at[k], r4.at[k], gpart(k))
        for k in range(1, 16)
    ]
    start(a4)
    partial = dot(gridT[...], fg[...])
    hpart[...] = partial
    hsnd[...] = partial.astype(BF16)
    a8 = [
        remote(hsnd.at[rows(lax.rem(x + k, 4), GP)], rcv8.at[k], s8.at[k], r8.at[k], xpart(k))
        for k in range(1, 4)
    ]
    start(a8)
    for i, k in enumerate(range(2, 16, 2)):
        arrived([zsend[i]])
        from_z = rows(lax.rem(gz - k + 16, 16), SLICE)
        zpass.append(remote(blocks.at[:, from_z], blocks.at[:, from_z], sC.at[k + 1], rC.at[k + 1], sibling))
        start(zpass[-1:])
    arrived(a4)
    v = ut[mine, :]
    for k in range(1, 16):
        v = v + rcv4[k].astype(F32)
    w = (jnp.where(x == 0, rootT_rhs[mine, :], 0.0) - v).astype(BF16)
    wsnd[...] = w
    rcv5[here] = w
    a5 = [remote(wsnd, rcv5.at[here], s5.at[k], r5.at[k], ppart(k)) for k in range(1, 16)]
    start(a5)
    arrived(gsend, y <= x)

    @pl.when(y <= x)
    def _():
        for a in range(4):
            bsnd[a] = dot(cg[a], lg[...]).astype(BF16)

    bsend = [
        remote(bsnd.at[lax.rem(x + k, 4)], rcvb.at[k], sB.at[k], rB.at[k], xpart(k)) for k in range(1, 4)
    ]
    start(bsend, y <= x)
    arrived(a8)
    hpart[my_piece, :] += rcv8[1].astype(F32) + rcv8[2].astype(F32) + rcv8[3].astype(F32)
    arrived(zpass)
    arrived(a5)
    res = []
    for j in range(4):
        t = rcv5[j].astype(F32)
        for i in range(1, 4):
            t = t + rcv5[i * 4 + j].astype(F32)
        res.append(t.astype(BF16))
    zs = []
    for i in range(4):
        t = dot_nt(res[0], blocks[i * (i + 1) // 2])
        for j in range(1, i + 1):
            t = t + dot_nt(res[j], blocks[i * (i + 1) // 2 + j])
        zs.append(t.astype(BF16))
    for j in range(4):
        t = dot(zs[j], blocks[j * (j + 1) // 2 + j])
        for i in range(j + 1, 4):
            t = t + dot(zs[i], blocks[i * (i + 1) // 2 + j])
        rt[mine, j * RB:(j + 1) * RB] = t.astype(BF16)

    a6 = [remote(rt.at[mine], rt.at[mine], s6.at[k], r6.at[k], gpart(k)) for k in range(2, 16, 2)]
    start(a6)
    a6b = [remote(rt.at[mine], rt.at[mine], s6.at[1], r6.at[1], sibling)]
    start(a6b)
    bacc[...] = jnp.zeros_like(bacc)

    @pl.when(y <= x)
    def _():
        bacc[...] = bsnd[x].astype(F32)

    for k in range(1, 4):
        sent = lax.rem(x - k + 4, 4) >= y
        arrived([bsend[k - 1]], sent)

        @pl.when(sent)
        def _():
            bacc[...] += rcvb[k].astype(F32)

    bm[...] = bacc[...].astype(BF16)
    btm[...] = bm[...].T
    bts[x] = btm[my_piece, :]
    at = [
        remote(btm.at[rows(lax.rem(x + k, 4), GP)], bts.at[x], sT.at[k], rT.at[k], xpart(k))
        for k in range(1, 4)
    ]
    start(at)
    for i, k in enumerate(range(2, 16, 2)):
        arrived([a6[i]])
        from_z = rows(lax.rem(gz - k + 16, 16), SLICE)
        a6b.append(
            remote(rt.at[from_z], rt.at[from_z], s6.at[k + 1], r6.at[k + 1], sibling)
        )
        start(a6b[-1:])
    arrived(at)
    arrived(a6b)
    h = hpart[my_piece, :]
    for i in range(4):
        h = h - dot_nt(bts[i], rt[:, i * RB:(i + 1) * RB])
    home = rows(y * 4 + x, GP)
    xg[home, :] = h.astype(BF16)
    a9 = [remote(xg.at[home], xg.at[home], s9.at[k], r9.at[k], ppart(k)) for k in range(1, 16)]
    start([a9[k - 1] for k in (4, 8, 12, 1, 3, 5, 7, 9, 11, 13, 15, 2, 6, 10, 14)])
    stores = [pltpu.make_async_copy(rt.at[:, rows(y, RB)], out_root, out_sems.at[2])]
    stores[0].start()
    odd = lax.rem(y, 2) == 1
    for k in range(1, 16):
        dy = k % 4
        if dy == 0:
            arrived(a9[k - 1:k])
        elif dy == 1:
            arrived(a9[k - 1:k], odd)
        elif dy == 3:
            arrived(a9[k - 1:k], jnp.logical_not(odd))
    top = pl.ds(pl.multiple_of((y // 2) * HALF, HALF), HALF)
    for g in range(2):
        ls = slice(g * 4, g * 4 + 4)
        t = dot(ct[ls, :, top].reshape(4 * N, HALF), xg[top, :])
        gs = slice(g * 4 * N, (g + 1) * 4 * N)
        ol[gs, :] = fl[gs, :].astype(F32) - t
    for k in range(1, 16):
        dy = k % 4
        if dy == 2:
            arrived(a9[k - 1:k])
        elif dy == 1:
            arrived(a9[k - 1:k], jnp.logical_not(odd))
        elif dy == 3:
            arrived(a9[k - 1:k], odd)
    rest = pl.ds(pl.multiple_of((1 - y // 2) * HALF, HALF), HALF)
    for g in range(2):
        gs = slice(g * 4 * N, (g + 1) * 4 * N)
        t = dot(ct[g * 4:g * 4 + 4, :, rest].reshape(4 * N, HALF), xg[rest, :])
        back[gs, :] = (ol[gs, :] - t).astype(BF16)
        stores.append(pltpu.make_async_copy(back.at[gs], out_back.at[gs], out_sems.at[g]))
        stores[-1].start()
    stores.append(pltpu.make_async_copy(xg.at[rows(y, GB)], out_top, out_sems.at[3]))
    stores[-1].start()
    finish()
    for c in stores:
        c.wait()


def leaves_back(
    inv_leaf, res_leaf, top, root, out_leaf, out_grid, out_root,
    il, bk, tp, rt, sol, og, oroot, i_sems, b_sems, sems,
):
    loads = []
    for l in range(NL):
        loads.append((
            pltpu.make_async_copy(inv_leaf.at[l], il.at[l], i_sems.at[l]),
            pltpu.make_async_copy(res_leaf.at[pl.ds(l * N, N)], bk.at[l], b_sems.at[l]),
        ))
        for c in loads[l]:
            c.start()
    small = [pltpu.make_async_copy(top, tp, sems.at[NL + 2]), pltpu.make_async_copy(root, rt, sems.at[NL + 3])]
    for c in small:
        c.start()
    copies = []
    for l in range(NL):
        for c in loads[l]:
            c.wait()
        sol[l] = dot_tn(il[l], bk[l])
        copies.append(pltpu.make_async_copy(sol.at[l], out_leaf.at[l], sems.at[l]))
        copies[-1].start()
    for c in small:
        c.wait()
    og[...] = tp[...].astype(F32)
    copies.append(pltpu.make_async_copy(og, out_grid.at[0], sems.at[NL]))
    copies[-1].start()
    oroot[...] = rt[...].astype(F32).T
    copies.append(pltpu.make_async_copy(oroot, out_root, sems.at[NL + 1]))
    copies[-1].start()
    for c in copies:
        c.wait()


def on_device(*args):
    vm = pltpu.VMEM
    dma = pltpu.SemaphoreType.DMA
    hbm = pl.BlockSpec(memory_space=pl.ANY)
    smem = pl.BlockSpec(memory_space=pltpu.SMEM)
    kept = pl.pallas_call(
        kernel,
        out_shape=(
            jax.ShapeDtypeStruct((NL * N, NRHS), BF16),
            jax.ShapeDtypeStruct((GB, NRHS), BF16),
            jax.ShapeDtypeStruct((NRHS, RB), BF16),
        ),
        in_specs=[hbm, hbm, hbm, smem, hbm, hbm, hbm, hbm, hbm],
        out_specs=(hbm, hbm, hbm),
        scratch_shapes=[
            vm((NL, N, NRHS), BF16), vm((NL, N, N), BF16), vm((NL, SG, N), BF16),
            vm((NL * N, NRHS), BF16), vm((NL, N, SG), BF16), vm((NL * N, NRHS), F32),
            vm((NL * N, NRHS), BF16), vm((SG, NRHS), BF16), vm((GB, GB), BF16), vm((GB, NRHS), BF16), vm((RB, NRHS), BF16),
            vm((4, RB, GB), BF16), vm((4, RB, GB), BF16), vm((4, RB, GB), BF16), vm((RB, GB), F32),
            vm((RB, GB), BF16), vm((GB, RB), BF16), vm((4, GP, RB), BF16),
            vm((GB, NRHS), F32), vm((SG, NRHS), BF16), vm((16, GP, NRHS), BF16),
            vm((GB, NRHS), BF16), vm((GB, NRHS), F32), vm((GB, NRHS), BF16),
            vm((4, GP, NRHS), BF16), vm((GB, NRHS), BF16), vm((GB, GB), BF16),
            vm((GB, NRHS), F32), vm((GB, NRHS), BF16), vm((4, GP, NRHS), BF16),
            vm((NRHS, RB), F32), vm((NRHS, RB), BF16), vm((16, SLICE, RB), BF16),
            vm((NRHS, RB), F32), vm((16, SLICE, RB), BF16), vm((SLICE, RB), BF16),
            vm((10, RB, RB), BF16), vm((NRHS, 4 * RB), BF16),
            dma((7,)), dma((4,)), dma((4,)),
            dma((16,)), dma((16,)), dma((4,)), dma((4,)), dma((4,)), dma((4,)), dma((4,)), dma((4,)),
            dma((16,)), dma((16,)), dma((16,)), dma((16,)), dma((16,)), dma((16,)),
            dma((4,)), dma((4,)), dma((16,)), dma((16,)),
            dma((16,)), dma((16,)), dma((16,)), dma((16,)), dma((4,)), dma((4,)), dma((4,)), dma((4,)),
            dma((4,)), dma((4,)),
        ],
        compiler_params=pltpu.CompilerParams(
            collective_id=0, has_side_effects=True, vmem_limit_bytes=62 << 20
        ),
        cost_estimate=pl.CostEstimate(flops=4_200_000_000, bytes_accessed=13_000_000, transcendentals=0),
        name="solve",
    )(*args)
    return pl.pallas_call(
        leaves_back,
        out_shape=(
            jax.ShapeDtypeStruct((NL, N, NRHS), F32),
            jax.ShapeDtypeStruct((1, GB, NRHS), F32),
            jax.ShapeDtypeStruct((RB, NRHS), F32),
        ),
        in_specs=[hbm] * 4,
        out_specs=(hbm, hbm, hbm),
        scratch_shapes=[
            vm((NL, N, N), BF16), vm((NL, N, NRHS), BF16), vm((GB, NRHS), BF16), vm((NRHS, RB), BF16),
            vm((NL, N, NRHS), F32), vm((GB, NRHS), F32), vm((RB, NRHS), F32),
            dma((NL,)), dma((NL,)), dma((NL + 4,)),
        ],
        compiler_params=pltpu.CompilerParams(vmem_limit_bytes=62 << 20),
        cost_estimate=pl.CostEstimate(flops=270_000_000, bytes_accessed=4_800_000, transcendentals=0),
        name="leaves_back",
    )(args[1], *kept)


def solution(mesh):
    return jax.shard_map(
        on_device,
        mesh=mesh,
        in_specs=(
            P(("gz", "row", "col"), None, None),
            P(("gz", "row", "col"), None, None),
            P(("gz", "row", "col"), None, None),
            P(("gz", "row", "col"), None),
            P("gz", "col", None),
            P("gz", "row", "col"),
            P("gz", "col", "row"),
            P("col", None),
            P("row", "col"),
        ),
        out_specs=(P(("gz", "row", "col"), None, None), P("gz", "col", None), P("col", None)),
        check_vma=False,
    )
```
